32 devices in a mesh: prompt: 4 (over z), slot: 8 (over y, x, core).
Axes of the slice: x: 2, y: 2, z: 4, core: 2. Of those that a mesh axis runs over, the one named last changes fastest.
Arguments:
- patch_kv: bfloat16 [4, 64, 128, 2048], P('prompt', 'slot'), may hold values from -6 to 6
- routes: int32 [4, 64], P('prompt', 'slot'), may hold values from -1 to 7, as said below
- prefix_kv: bfloat16 [4, 512, 2048], P('prompt', None, 'slot'), may hold values from -4 to 4
- prefix_len: int32 [4], P('prompt'), may hold values from 1 to 512, 1536 in all
- queries: bfloat16 [4, 8, 256, 8192], P('prompt', 'slot'), may hold values from -160 to 160
- suffix_kv: bfloat16 [4, 8, 256, 2048], P('prompt', 'slot'), may hold values from -6 to 6
- score_head: float32 [8192], replicated, may hold values from -0.0625 to 0.0625
Outputs:
- context: bfloat16 [4, 8, 256, 8192], P('prompt', 'slot')
- advantage: float32 [4, 8], P('prompt', 'slot')
The draws below stay inside these ranges and needn't reach their ends.
Inputs may be any that keep to these rules, and one draw needn't show every extreme that they name: `routes`: in the list of one generating device each judge index appears at most once, and in one prompt's lists each judge index appears exactly 4 times; -1 marks an empty slot.
All inputs are finite; a program needn't handle non-finite values. No bound on the sum of `prefix_len` on one device may be relied on, other than what follows from the above.
Results may differ from the reference program's by a relative error of at most 0.005.
Values may be sent and summed in bfloat16 or wider, within the bound.
No kernel may reach another device: no remote copies, remote signals or barrier semaphores. Data moves between devices by JAX's collectives and lax.ppermute only.
A program may use at most 128 MiB of HBM per device.

```python
import math
import jax
import jax.numpy as jnp
import numpy as np
from jax import lax

HEADS = 64
KVH = 8
HD = 128
PREFIX = 512
SUF = 256
TILE = 128
PROMPTS = 4
IMG_TILES = 4
IMG = 512
KVW = 2048
QW = 8192
N_SLOT = 8


def prefix_values(key):
    values = jax.random.normal(jax.random.fold_in(key, 11), (PROMPTS, PREFIX, KVW), jnp.float32)
    return jnp.clip(values, -4.0, 4.0)


def draw_prefix_kv(key, part):
    return prefix_values(key).astype(jnp.bfloat16)


def draw_queries(key, part):
    values = jax.random.normal(jax.random.fold_in(key, 12), (PROMPTS, N_SLOT, SUF, HEADS * HD), jnp.float32)
    values = jnp.clip(values, -6.0, 6.0)
    return values.astype(jnp.bfloat16)


def draw_routes(key, part):

    def one_prompt(prompt_key):
        judge_keys = jax.random.split(jax.random.fold_in(prompt_key, 1), N_SLOT)
        senders = jax.vmap(lambda k: jax.random.permutation(k, N_SLOT))(judge_keys)
        ranking = jnp.argsort(senders, axis=1)
        chosen = ranking < N_SLOT // 2
        source_keys = jax.random.split(jax.random.fold_in(prompt_key, 2), N_SLOT)
        layout = jax.vmap(lambda k: jax.random.permutation(k, N_SLOT))(source_keys)
        sources = jnp.arange(N_SLOT)[:, None]
        taken = chosen[layout, sources]
        return jnp.where(taken, layout, -1).reshape(N_SLOT * N_SLOT)
    prompt_keys = jax.random.split(jax.random.fold_in(key, 13), PROMPTS)
    return jax.vmap(one_prompt)(prompt_keys).astype(jnp.int32)


def block_levels(own_key, dims, cuts, low, largest):
    level, own = 1.0, jax.random.fold_in(own_key, 6)
    for axis_at, blocks in cuts:
        draws = jnp.exp(jax.random.uniform(jax.random.fold_in(own, axis_at), (blocks,), jnp.float32, low / len(cuts), largest / len(cuts)))
        level = level * jnp.repeat(draws, dims[axis_at] // blocks).reshape([-1 if axis == axis_at else 1 for axis in range(len(dims))])
    return level


def length_profile(number_of, total, reach, slope):
    loads = [(1 << 20) // math.isqrt(standing ** slope) + 1 for standing in range(2, number_of + 1)]
    rest, counts = total - reach - (number_of - 1), [1] * (number_of - 1)
    while rest > 0:
        movable = [i for i in range(number_of - 1) if counts[i] < reach]
        mass, budget = sum([loads[i] for i in movable]), rest
        for i in movable:
            addition = min(reach - counts[i], max(1, budget * loads[i] // mass), rest)
            counts[i] = counts[i] + addition
            rest = rest - addition
    return np.array([reach] + counts)


def ragged(stream_key, count, total, bound, lean):
    if count == 2:
        one = jax.random.randint(stream_key, (), max(1, total - bound), min(bound, total - 1) + 1)
        return jnp.stack([one, total - one])
    lengths = jnp.asarray(length_profile(count, total, bound, lean), jnp.int32)
    couples = (count - 1) // 2
    source_of, taker = lengths[1:1 + 2 * couples:2], lengths[2:2 + 2 * couples:2]
    margin = jnp.minimum(source_of - 1, bound - taker)
    shifted = jax.random.randint(jax.random.fold_in(stream_key, 1), (couples,), 0, 1 << 20) % (margin + 1)
    lengths = lengths.at[1:1 + 2 * couples:2].set(source_of - shifted).at[2:2 + 2 * couples:2].set(taker + shifted)
    return lengths[jax.random.permutation(jax.random.fold_in(stream_key, 2), count)]


def centred(key, shape, scale, limit, cuts=(), kind=jnp.bfloat16):
    level = block_levels(key, shape, cuts, -0.22, 0.18) if cuts else 1.0
    values = jax.random.normal(key, shape, jnp.float32) * scale * level
    return jnp.minimum(jnp.maximum(values, -limit), limit).astype(kind)


def setup_inputs(seed: int = 0) -> dict:
    splits = jax.random.split(jax.random.key(seed), 8)
    patch_kv = centred(splits[0], (PROMPTS, N_SLOT * N_SLOT, TILE, KVW), 1.0, 6.0, ((0, 4), (1, 8)))
    routes = draw_routes(jax.random.fold_in(splits[7], 71), 0)
    prefix_kv = draw_prefix_kv(jax.random.fold_in(splits[7], 71), 0)
    prefix_len = ragged(splits[3], PROMPTS, PROMPTS * PREFIX * 3 // 4, PREFIX, 1).astype(jnp.int32)
    queries = draw_queries(jax.random.fold_in(splits[7], 71), 0)
    suffix_kv = centred(splits[5], (PROMPTS, N_SLOT, SUF, KVW), 1.0, 6.0, ((0, 4), (1, 8)))
    score_head = centred(splits[6], (QW,), QW ** -0.5, 0.0625, (), jnp.float32)
    return {"patch_kv": patch_kv, "routes": routes, "prefix_kv": prefix_kv, "prefix_len": prefix_len, "queries": queries, "suffix_kv": suffix_kv, "score_head": score_head}


def head_attention(query_rows, key_rows, value_rows, allowed):
    factor = 1.0 / math.sqrt(HD)
    scores = jnp.einsum('sgd,kd->gsk', query_rows.astype(jnp.float32), key_rows.astype(jnp.float32)) * factor
    scores = jnp.where(allowed[None, :, :], scores, -1e+30)
    peak = lax.optimization_barrier(jnp.max(scores, axis=-1, keepdims=True))
    weights = jnp.exp(scores - peak)
    totals = lax.optimization_barrier(jnp.sum(weights, axis=-1))
    rounded = weights.astype(jnp.bfloat16)
    mixed = jnp.einsum('gsk,kd->sgd', rounded.astype(jnp.float32), value_rows.astype(jnp.float32))
    return mixed / jnp.transpose(totals)[:, :, None]

def reference(patch_kv, routes, prefix_kv, prefix_len, queries, suffix_kv, score_head):
    groups = HEADS // KVH

    def one_image(pair):
        prompt = pair[0]
        judge = pair[1]
        found = jnp.nonzero(routes[prompt] == judge, size=IMG_TILES)[0].astype(jnp.int32)
        image_rows = patch_kv[prompt][found].reshape(IMG, KVW)
        rows_all = jnp.concatenate([prefix_kv[prompt], image_rows, suffix_kv[prompt, judge]], axis=0)
        columns = jnp.arange(PREFIX + IMG + SUF, dtype=jnp.int32)[None, :]
        positions = jnp.arange(SUF, dtype=jnp.int32)[:, None]
        allowed = jnp.where(columns < PREFIX, columns < prefix_len[prompt], jnp.where(columns < PREFIX + IMG, True, columns - PREFIX - IMG <= positions))
        own_queries = queries[prompt, judge]
        pieces = []
        for group in range(KVH):
            query_rows = own_queries[:, group * groups * HD:(group + 1) * groups * HD].reshape(SUF, groups, HD)
            key_rows = rows_all[:, group * HD:(group + 1) * HD]
            value_rows = rows_all[:, (KVH + group) * HD:(KVH + group + 1) * HD]
            pieces.append(head_attention(query_rows, key_rows, value_rows, allowed).reshape(SUF, groups * HD))
        return jnp.concatenate(pieces, axis=1).astype(jnp.bfloat16)
    prompt_ids = jnp.repeat(jnp.arange(PROMPTS, dtype=jnp.int32), N_SLOT)
    judge_ids = jnp.tile(jnp.arange(N_SLOT, dtype=jnp.int32), PROMPTS)
    context = lax.map(one_image, jnp.stack([prompt_ids, judge_ids], axis=1))
    context = context.reshape(PROMPTS, N_SLOT, SUF, HEADS * HD)
    last_rows = context[:, :, SUF - 1, :].astype(jnp.float32).reshape(PROMPTS * N_SLOT, HEADS * HD)
    score = jnp.dot(last_rows, score_head, precision=lax.Precision.HIGHEST, preferred_element_type=jnp.float32).reshape(PROMPTS, N_SLOT)
    centre = lax.optimization_barrier(jnp.sum(score, axis=1, keepdims=True)) / N_SLOT
    deviation = score - centre
    spread = jnp.sum(deviation * deviation) / (PROMPTS * N_SLOT)
    advantage = deviation / jnp.sqrt(spread + 1e-06)
    return (context, advantage)
```

```python
import functools
import math

import jax
import jax.numpy as jnp
from jax import lax
from jax.experimental import pallas as pl
from jax.experimental.pallas import tpu as pltpu
from jax.sharding import PartitionSpec as P

HEADS = 64
KVH = 8
HD = 128
GROUPS = HEADS // KVH
SCALE = math.log2(math.e) / math.sqrt(HD)
LOW = -1e30
EXTRA = 16
NT = (((1,), (1,)), ((), ()))
VMEM_LIMIT = 56 * 2**20


def pack_kernel(head_from, heads, chips, routes_ref, patch_ref, *rest):
    outs, sem = rest[:chips], rest[chips]
    slots = patch_ref.shape[0]
    me = lax.axis_index("slot")
    chip, core = me // 2, me % 2
    width = heads * HD
    copies = []
    for offset in range(chips):
        for other in range(2):
            judge = 2 * (chip ^ offset) + (core ^ other)
            tile = jnp.int32(0)
            for s in range(slots):
                tile = jnp.where(routes_ref[s] == judge, s, tile)
            for half in range(2):
                copies.append(
                    pltpu.make_async_copy(
                        patch_ref.at[tile, :, pl.ds((half * KVH + head_from) * HD, width)],
                        outs[offset].at[other, :, pl.ds(half * width, width)],
                        sem.at[len(copies)],
                    )
                )
    for copy in copies:
        copy.start()
    for copy in copies:
        copy.wait()


def pack(head_from, heads, chips, routes, patch):
    rows = patch.shape[1]
    shape = jax.ShapeDtypeStruct((2, rows, 2 * heads * HD), patch.dtype)
    return pl.pallas_call(
        functools.partial(pack_kernel, head_from, heads, chips),
        out_shape=[shape] * chips,
        in_specs=[pl.BlockSpec(memory_space=pltpu.SMEM), pl.BlockSpec(memory_space=pl.ANY)],
        out_specs=[pl.BlockSpec(memory_space=pl.ANY)] * chips,
        scratch_shapes=[pltpu.SemaphoreType.DMA((4 * chips,))],
        cost_estimate=pl.CostEstimate(
            flops=0, bytes_accessed=chips * 8 * rows * heads * HD * 2, transcendentals=0
        ),
        name="pack_tiles",
    )(routes, patch)


def prefix_kernel(chips, *rest):
    near, far, out, sem = rest[:chips], rest[chips], rest[chips + 1], rest[chips + 2]
    rows, columns = out.shape[0], near[0].shape[1]
    me = lax.axis_index("slot")
    chip, core = me // 2, me % 2
    copies = []
    for offset in range(chips):
        for other in range(2):
            owner = 2 * (chip ^ offset) + (core ^ other)
            source = near[offset] if other == 0 else far.at[offset]
            copies.append(
                pltpu.make_async_copy(
                    source.at[pl.ds(0, rows), :],
                    out.at[:, pl.ds(pl.multiple_of(owner * columns, 128), columns)],
                    sem.at[len(copies)],
                )
            )
    for copy in copies:
        copy.start()
    for copy in copies:
        copy.wait()


def join_prefix(chips, rows, near, far):
    width = 2 * chips * near[0].shape[1]
    return pl.pallas_call(
        functools.partial(prefix_kernel, chips),
        out_shape=jax.ShapeDtypeStruct((rows, width), near[0].dtype),
        in_specs=[pl.BlockSpec(memory_space=pl.ANY)] * (chips + 1),
        out_specs=pl.BlockSpec(memory_space=pl.ANY),
        scratch_shapes=[pltpu.SemaphoreType.DMA((2 * chips,))],
        cost_estimate=pl.CostEstimate(flops=0, bytes_accessed=rows * width * 4, transcendentals=0),
        name="join_prefix",
    )(*near, far)


def attention_kernel(chips, kept, aliased, meta_ref, head_ref, q_ref, pk_ref, pv_ref, sk_ref, sv_ref, *rest):
    tiles = rest[: 4 * chips]
    rest = rest[4 * chips + (1 if aliased else 0) :]
    o_ref, score_ref, kbuf, vbuf = rest
    slots = 2 * chips
    prefix_rows, suffix_rows = pk_ref.shape[0], sk_ref.shape[0]
    tile_rows = tiles[0].shape[1]
    start = prefix_rows + kept * tile_rows
    total = start + suffix_rows
    length = meta_ref[2 * slots]

    @pl.when(pl.program_id(0) == 0)
    def _():
        score_ref[...] = jnp.zeros_like(score_ref)

    live = lax.broadcasted_iota(jnp.int32, (prefix_rows, HD), 0) < length
    kbuf[:prefix_rows] = jnp.where(live, pk_ref[...], pk_ref[0:1, :])
    vbuf[:prefix_rows, :HD] = jnp.where(live, pv_ref[...], jnp.zeros_like(pv_ref[...]))
    vbuf[:prefix_rows, HD:] = live.astype(vbuf.dtype)
    vbuf[prefix_rows:, HD:] = jnp.ones((total - prefix_rows, HD), vbuf.dtype)
    kbuf[start:] = sk_ref[...]
    vbuf[start:, :HD] = sv_ref[...]
    for n in range(slots):
        @pl.when(meta_ref[n] > 0)
        def _(n=n):
            row = pl.multiple_of(prefix_rows + meta_ref[slots + n] * tile_rows, tile_rows)
            kbuf[pl.ds(row, tile_rows), :] = tiles[2 * n][0]
            vbuf[pl.ds(row, tile_rows), :HD] = tiles[2 * n + 1][0]

    causal = lax.broadcasted_iota(jnp.int32, (suffix_rows, suffix_rows), 1) <= lax.broadcasted_iota(
        jnp.int32, (suffix_rows, suffix_rows), 0
    )

    def scores(h):
        s = lax.dot_general(
            q_ref[:, h * HD : (h + 1) * HD], kbuf[...], NT, preferred_element_type=jnp.float32
        )
        return jnp.concatenate([s[:, :start], jnp.where(causal, s[:, start:], LOW)], axis=1)

    def finish(s, h):
        peak = jnp.max(s, axis=1, keepdims=True)
        weights = jnp.exp2((s - peak) * SCALE).astype(jnp.bfloat16)
        mixed = jnp.dot(weights, vbuf[...], preferred_element_type=jnp.float32)
        out = (mixed[:, :HD] / mixed[:, HD:]).astype(o_ref.dtype)
        o_ref[:, h * HD : (h + 1) * HD] = out
        last = out[suffix_rows - 8 :, :].astype(jnp.float32)
        score_ref[...] += last * head_ref[0:1, h * HD : (h + 1) * HD]

    held = scores(0)
    for h in range(1, GROUPS):
        following = scores(h)
        finish(held, h - 1)
        held = following
    finish(held, GROUPS - 1)


def attend(chips, kept, head_from, heads, meta, head, queries, prefix, suffix, near, far, context):
    rows = queries.shape[0]
    prefix_rows, suffix_rows = prefix.shape[0], suffix.shape[0]
    tile_rows = near[0].shape[1]
    total = prefix_rows + kept * tile_rows + suffix_rows
    wide = GROUPS * HD
    column = lambda shift: (lambda g: (0, head_from + shift + g))
    specs = [
        pl.BlockSpec(memory_space=pltpu.SMEM),
        pl.BlockSpec((1, wide), column(0)),
        pl.BlockSpec((rows, wide), column(0)),
        pl.BlockSpec((prefix_rows, HD), column(0)),
        pl.BlockSpec((prefix_rows, HD), column(KVH)),
        pl.BlockSpec((suffix_rows, HD), column(0)),
        pl.BlockSpec((suffix_rows, HD), column(KVH)),
    ]
    operands = [meta, head, queries, prefix, prefix, suffix, suffix]
    for offset in range(chips):
        for other in range(2):
            array, place = (near[offset], 0) if other == 0 else (far, offset)
            for half in range(2):
                specs.append(
                    pl.BlockSpec(
                        (1, tile_rows, HD), lambda g, p=place, s=half * heads: (p, 0, s + g)
                    )
                )
                operands.append(array)
    aliases = {}
    if context is not None:
        aliases = {len(operands): 0}
        specs.append(pl.BlockSpec(memory_space=pl.ANY))
        operands.append(context)
    return pl.pallas_call(
        functools.partial(attention_kernel, chips, kept, context is not None),
        grid=(heads,),
        out_shape=[
            jax.ShapeDtypeStruct(queries.shape, queries.dtype),
            jax.ShapeDtypeStruct((8, HD), jnp.float32),
        ],
        in_specs=specs,
        out_specs=[
            pl.BlockSpec((rows, wide), column(0)),
            pl.BlockSpec((8, HD), lambda g: (0, 0)),
        ],
        scratch_shapes=[
            pltpu.VMEM((total, HD), queries.dtype),
            pltpu.VMEM((total, 2 * HD), queries.dtype),
        ],
        input_output_aliases=aliases,
        compiler_params=pltpu.CompilerParams(vmem_limit_bytes=VMEM_LIMIT),
        cost_estimate=pl.CostEstimate(
            flops=heads * GROUPS * rows * total * HD * 8,
            bytes_accessed=heads * (rows * wide * 4 + total * HD * 4),
            transcendentals=heads * GROUPS * rows * total,
        ),
        name="attend",
    )(*operands)


def per_device(patch_kv, routes, prefix_kv, prefix_len, queries, suffix_kv, score_head):
    slot_count = lax.axis_size("slot")
    prompt_count = lax.axis_size("prompt")
    chips = slot_count // 2
    kept = slot_count // 2
    slots = routes.shape[1]
    prefix_rows, prefix_columns = prefix_kv.shape[1:]
    me = lax.axis_index("slot")
    chip, core = me // 2, me % 2

    def swap(x, k):
        return lax.ppermute(x, "slot", [(i, i ^ k) for i in range(slot_count)])

    listed = jnp.pad(routes.astype(jnp.bfloat16), ((0, EXTRA - 1), (0, prefix_columns - slots)))
    block = jnp.concatenate([prefix_kv[0], listed], axis=0)
    near = [block] + [swap(block, 2 * offset) for offset in range(1, chips)]
    far = swap(jnp.stack(near), 1)
    lists = [part for offset in range(chips) for part in (near[offset], far[offset])]
    lists = jnp.stack([part[prefix_rows, :slots] for part in lists]).astype(jnp.int32)
    present = jnp.any(lists == me, axis=1).astype(jnp.int32)
    meta = jnp.concatenate([present, jnp.cumsum(present) - present, prefix_len]).astype(jnp.int32)
    prefix = join_prefix(chips, prefix_rows, near, far)

    parts = ((0, 3), (3, 2), (5, 2), (7, 1))
    arrived = []
    for n, (head_from, heads) in enumerate(parts):
        buffers = pack(head_from, heads, chips, routes[0], patch_kv[0])
        if n >= 2:
            buffers = list(lax.optimization_barrier((tuple(buffers), arrived[n - 2][0]))[0])
        got = [buffers[0]] + [swap(buffers[offset], 2 * offset) for offset in range(1, chips)]
        passed = swap(jnp.stack([part[1] for part in got]), 1)
        arrived.append((got, passed))

    head = score_head.reshape(1, -1)
    context, shares = None, []
    for (head_from, heads), (got, passed) in zip(parts, arrived):
        context, share = attend(
            chips, kept, head_from, heads, meta, head, queries[0, 0], prefix, suffix_kv[0, 0],
            got, passed, context,
        )
        shares.append(share[7])
    score = jnp.sum(sum(shares)).reshape(1)

    pair = jnp.concatenate([score, swap(score, 1)])
    every = jnp.concatenate([pair] + [swap(pair, 2 * offset) for offset in range(1, chips)])
    centre = jnp.sum(every) / slot_count
    own = jnp.sum((every - centre) ** 2).reshape(1)
    squares = own
    for k in range(1, prompt_count):
        squares = squares + lax.ppermute(own, "prompt", [(i, i ^ k) for i in range(prompt_count)])
    spread = squares / (prompt_count * slot_count)
    advantage = (score - centre) / jnp.sqrt(spread + 1e-06)
    return (context[None, None], advantage.reshape(1, 1))


def solution(mesh):
    placed = (
        P("prompt", "slot", None, None),
        P("prompt", "slot"),
        P("prompt", None, "slot"),
        P("prompt"),
        P("prompt", "slot", None, None),
        P("prompt", "slot", None, None),
        P(),
    )
    return jax.shard_map(
        per_device,
        mesh=mesh,
        in_specs=placed,
        out_specs=(P("prompt", "slot", None, None), P("prompt", "slot")),
        check_vma=False,
    )
```

```python
import functools
import math

import jax
import jax.numpy as jnp
from jax import lax
from jax.experimental import pallas as pl
from jax.experimental.pallas import tpu as pltpu
from jax.sharding import PartitionSpec as P

HEADS = 64
KVH = 8
HD = 128
GROUPS = HEADS // KVH
SCALE = math.log2(math.e) / math.sqrt(HD)
LOW = -1e30
ROOM = 100.0
PARTS = ((0, 6, True), (6, 2, False))
LAST = 16
EMPTY = 1024.0
NT = (((1,), (1,)), ((), ()))
VMEM_LIMIT = 56 * 2**20


def lasting(microseconds):
    return pl.CostEstimate(flops=0, bytes_accessed=int(microseconds * 3.5e6), transcendentals=0)


PARAMS = pltpu.CompilerParams(vmem_limit_bytes=VMEM_LIMIT)


def slot_of(judge, routes):
    tile, found = jnp.int32(0), jnp.bool_(False)
    for s in range(routes.shape[0]):
        here = routes[s] == judge
        tile, found = jnp.where(here, s, tile), found | here
    return tile, found


def pack_kernel(chips, parts, me, routes, mate_routes, *rest):
    tiles, outs = rest[: 2 * chips], list(rest[2 * chips :])
    chip, core = me[0] // 2, me[0] % 2
    top = (lax.broadcasted_iota(jnp.int32, (16, HD), 0) == 0) & (pl.program_id(0) == 0)
    for head_from, heads, together in parts:
        width = heads * HD
        for offset in range(chips):
            out = outs[0].at[chip ^ offset] if together else outs.pop(0)
            for n, held in enumerate((routes, mate_routes)):
                tile = tiles[2 * offset + n]
                found = slot_of(2 * (chip ^ offset) + core, held)[1]
                for half in range(2):
                    first = (half * KVH + head_from) * HD
                    out[n, :, half * width : (half + 1) * width] = tile[0, :, first : first + width]
                mark = top & jnp.logical_not(found)
                kept = tile[0, :16, head_from * HD : (head_from + 1) * HD]
                out[n, :16, :HD] = jnp.where(mark, jnp.full_like(kept, EMPTY), kept)
        if together:
            outs.pop(0)


def pack(parts, chips, me, routes, mate_routes, patch, mate_patch):
    tile_rows, width = patch.shape[1:]
    rows = tile_rows // 4
    shapes, specs, sources = [], [], []
    for _, heads, together in parts:
        shape = (2, tile_rows, 2 * heads * HD)
        block = (2, rows, 2 * heads * HD)
        if together:
            shapes.append((chips,) + shape)
            specs.append(pl.BlockSpec((chips,) + block, lambda r, *_: (0, 0, r, 0)))
        else:
            shapes += [shape] * chips
            specs += [pl.BlockSpec(block, lambda r, *_: (0, r, 0))] * chips
    for offset in range(chips):
        for n in range(2):

            def source(r, me, *held, offset=offset, n=n):
                judge = 2 * ((me[0] // 2) ^ offset) + me[0] % 2
                return slot_of(judge, held[n])[0], r, 0

            sources.append(pl.BlockSpec((1, rows, width), source))
    return pl.pallas_call(
        functools.partial(pack_kernel, chips, parts),
        out_shape=[jax.ShapeDtypeStruct(shape, patch.dtype) for shape in shapes],
        grid_spec=pltpu.PrefetchScalarGridSpec(
            num_scalar_prefetch=3,
            grid=(tile_rows // rows,),
            in_specs=sources,
            out_specs=specs,
        ),
        compiler_params=PARAMS,
        cost_estimate=lasting(5),
        name="pack_tiles",
    )(me, routes, mate_routes, *([patch, mate_patch] * chips))


def pipelined(scores, finish):
    held = scores(0)
    for h in range(1, GROUPS):
        following = scores(h)
        finish(held, h - 1)
        held = following
    finish(held, GROUPS - 1)


def text_kernel(
    per_slot, me, length, q_ref, kn_ref, kf_ref, vn_ref, vf_ref, sk_ref, sv_ref, o_ref, stat_ref,
    kbuf, vbuf,
):
    prefix_rows, suffix_rows = kn_ref.shape[1], sk_ref.shape[0]
    g = pl.program_id(0)
    live = lax.broadcasted_iota(jnp.int32, (prefix_rows, HD), 0) < length[0]

    @pl.when(g == 0)
    def _():
        vbuf[:prefix_rows, HD:] = live.astype(vbuf.dtype)
        vbuf[prefix_rows:, HD:] = jnp.ones((suffix_rows, HD), vbuf.dtype)

    def held_by(head, near, far):
        return jnp.where((head // per_slot) % 2 == me[0] % 2, near[0], far[0])

    keys = held_by(g, kn_ref, kf_ref)
    values = held_by(KVH + g, vn_ref, vf_ref)
    kbuf[:prefix_rows] = jnp.where(live, keys, keys[0:1, :])
    vbuf[:prefix_rows, :HD] = jnp.where(live, values, jnp.zeros_like(values))
    kbuf[prefix_rows:] = sk_ref[...]
    vbuf[prefix_rows:, :HD] = sv_ref[...]
    causal = lax.broadcasted_iota(jnp.int32, (suffix_rows, suffix_rows), 1) <= lax.broadcasted_iota(
        jnp.int32, (suffix_rows, suffix_rows), 0
    )
    def scores(h):
        s = lax.dot_general(
            q_ref[:, h * HD : (h + 1) * HD], kbuf[...], NT, preferred_element_type=jnp.float32
        )
        return jnp.concatenate(
            [s[:, :prefix_rows], jnp.where(causal, s[:, prefix_rows:], LOW)], axis=1
        )

    def finish(s, h):
        peak = jnp.max(s, axis=1, keepdims=True) * SCALE
        weights = jnp.exp2(s * SCALE - peak).astype(jnp.bfloat16)
        mixed = jnp.dot(weights, vbuf[...], preferred_element_type=jnp.float32)
        o_ref[:, h * HD : (h + 1) * HD] = mixed[:, :HD]
        stat_ref[:, h : h + 1] = peak
        stat_ref[:, GROUPS + h : GROUPS + h + 1] = mixed[:, HD : HD + 1]

    pipelined(scores, finish)


def attend_text(me, length, queries, near, far, suffix):
    rows = queries.shape[0]
    prefix_rows, suffix_rows = near.shape[1], suffix.shape[0]
    per_slot = near.shape[2] // HD
    total, wide = prefix_rows + suffix_rows, GROUPS * HD

    def block(shift):
        def index(g, me, length):
            head = shift + g
            return (head // per_slot // 2) ^ (me[0] // 2), 0, head % per_slot

        return pl.BlockSpec((1, prefix_rows, HD), index)

    return pl.pallas_call(
        functools.partial(text_kernel, per_slot),
        out_shape=[
            jax.ShapeDtypeStruct(queries.shape, jnp.float32),
            jax.ShapeDtypeStruct((rows, KVH * HD), jnp.float32),
        ],
        grid_spec=pltpu.PrefetchScalarGridSpec(
            num_scalar_prefetch=2,
            grid=(KVH,),
            in_specs=[
                pl.BlockSpec((rows, wide), lambda g, me, length: (0, g)),
                block(0),
                block(0),
                block(KVH),
                block(KVH),
                pl.BlockSpec((suffix_rows, HD), lambda g, me, length: (0, g)),
                pl.BlockSpec((suffix_rows, HD), lambda g, me, length: (0, KVH + g)),
            ],
            out_specs=[
                pl.BlockSpec((rows, wide), lambda g, me, length: (0, g)),
                pl.BlockSpec((rows, HD), lambda g, me, length: (0, g)),
            ],
            scratch_shapes=[
                pltpu.VMEM((total, HD), queries.dtype),
                pltpu.VMEM((total, 2 * HD), queries.dtype),
            ],
        ),
        compiler_params=PARAMS,
        cost_estimate=lasting(21),
        name="attend_text",
    )(me, length, queries, near, far, near, far, suffix, suffix)


def image_kernel(
    chips, kept, together, chained, stored, scored, head_ref, q_ref, acc_ref, stat_ref, *rest
):
    rest = list(rest)
    tiles = [rest.pop(0) for _ in range(1 if together else chips)]
    before = rest.pop(0) if chained and scored else None
    if chained and stored:
        rest.pop(0)
    o_ref = rest.pop(0) if stored else None
    score_ref = rest.pop(0) if scored else None
    kbuf, vbuf, gain_ref, place_ref = rest
    slots = 2 * chips
    rows = q_ref.shape[0]
    tile_rows, width = tiles[0].shape[-2], tiles[0].shape[-1] // 2
    total = kept * tile_rows
    g = pl.program_id(0)

    @pl.when(g == 0)
    def _():
        gain_ref[...] = before[...] if before is not None else jnp.zeros_like(gain_ref)
        vbuf[:, HD:] = jnp.ones((total + tile_rows, HD), vbuf.dtype)
        count = jnp.int32(0)
        for n in range(slots):
            tile = tiles[0].at[n // 2, n % 2] if together else tiles[n // 2].at[n % 2]
            found = jnp.max(tile[0:1, :HD].astype(jnp.float32)) < EMPTY
            place_ref[n] = jnp.where(found, count, kept)
            count = count + jnp.where(found, 1, 0)

    for n in range(slots):
        row = pl.multiple_of(place_ref[n] * tile_rows, tile_rows)
        tile = tiles[0].at[n // 2, n % 2] if together else tiles[n // 2].at[n % 2]
        column = pl.ds(pl.multiple_of(g * HD, HD), HD)
        kbuf[pl.ds(row, tile_rows), :] = tile[:, column]
        column = pl.ds(pl.multiple_of(width + g * HD, HD), HD)
        vbuf[pl.ds(row, tile_rows), :HD] = tile[:, column]

    def scores(column):
        return lax.dot_general(
            q_ref[:, column], kbuf[:total], NT, preferred_element_type=jnp.float32
        )

    def close(summed, totals, column):
        out = (summed / totals).astype(jnp.bfloat16)
        if stored:
            o_ref[:, column] = out
        last = out[rows - 8 :, :].astype(jnp.float32)
        return last * head_ref[0:1, column] if scored else 0.0

    gains = [jnp.zeros((8, HD), jnp.float32), jnp.full((8, HD), LOW, jnp.float32)]

    def finish(s, h):
        column = slice(h * HD, (h + 1) * HD)
        held = stat_ref[:, h : h + 1]
        powers = []
        for k in range(total // HD):
            power = s[:, k * HD : (k + 1) * HD] * SCALE - held
            gains[1] = jnp.maximum(gains[1], jnp.max(power.reshape(rows // 8, 8, HD), axis=0))
            powers.append(jnp.exp2(power).astype(jnp.bfloat16))
        weights = jnp.concatenate(powers, axis=1)
        mixed = jnp.dot(weights, vbuf[:total], preferred_element_type=jnp.float32)
        totals = mixed[:, HD:] + stat_ref[:, GROUPS + h : GROUPS + h + 1]
        gains[0] = gains[0] + close(mixed[:, :HD] + acc_ref[:, column], totals, column)

    pipelined(lambda h: scores(slice(h * HD, (h + 1) * HD)), finish)
    fits = jnp.max(gains[1]) < ROOM

    if scored:
        @pl.when(fits)
        def _():
            gain_ref[...] += gains[0]

    @pl.when(jnp.logical_not(fits))
    def _():
        def one(h, gain):
            column = pl.ds(pl.multiple_of(h * HD, HD), HD)
            s = scores(column) * SCALE
            lane = lax.broadcasted_iota(jnp.int32, (rows, HD), 1)
            held = jnp.sum(jnp.where(lane == h, stat_ref[...], 0.0), axis=1, keepdims=True)
            sums = jnp.where(lane == GROUPS + h, stat_ref[...], 0.0)
            sums = jnp.sum(sums, axis=1, keepdims=True)
            peak = jnp.maximum(held, jnp.max(s, axis=1, keepdims=True))
            weights = jnp.exp2(s - peak).astype(jnp.bfloat16)
            mixed = jnp.dot(weights, vbuf[:total], preferred_element_type=jnp.float32)
            fade = jnp.exp2(held - peak)
            summed = acc_ref[:, column] * fade + mixed[:, :HD]
            totals = sums * fade + mixed[:, HD:]
            return gain + close(summed, totals, column)

        gain = lax.fori_loop(0, GROUPS, one, jnp.zeros((8, HD), jnp.float32))
        if scored:
            gain_ref[...] += gain

    if scored:
        @pl.when(g == pl.num_programs(0) - 1)
        def _():
            if stored:
                score_ref[...] = gain_ref[...]
            else:
                score_ref[...] = jnp.broadcast_to(gain_ref[7:8, :], score_ref.shape)


def attend_image(
    chips, kept, part, head, queries, text, tiles, context=None, share=None, devices=0
):
    head_from, heads, together = part
    stored, scored = devices == 0, devices > 0 or context is None
    chained = context is not None or share is not None
    all_rows = queries.shape[0]
    rows = all_rows if stored else LAST
    tile_rows = tiles[0].shape[-2]
    total, wide = kept * tile_rows, GROUPS * HD
    column = lambda g: (all_rows // rows - 1, head_from + g)
    fixed = lambda g: (0, 0)
    specs = [
        pl.BlockSpec((1, wide), lambda g: (0, head_from + g)),
        pl.BlockSpec((rows, wide), column),
        pl.BlockSpec((rows, wide), column),
        pl.BlockSpec((rows, HD), column),
    ] + [pl.BlockSpec(memory_space=pltpu.VMEM) for tile in tiles]
    operands = [head, queries, *text, *tiles]
    aliases, shapes, outs = {}, [], []
    if chained and scored:
        specs.append(pl.BlockSpec((8, HD), fixed))
        operands.append(share)
    if chained and stored:
        aliases = {len(operands): 0}
        specs.append(pl.BlockSpec(memory_space=pl.ANY))
        operands.append(context)
    if stored:
        shapes.append(jax.ShapeDtypeStruct(queries.shape, queries.dtype))
        outs.append(pl.BlockSpec((rows, wide), column))
    if scored:
        shape = (8 if stored else devices, HD)
        shapes.append(jax.ShapeDtypeStruct(shape, jnp.float32))
        outs.append(pl.BlockSpec(shape, fixed))
    return pl.pallas_call(
        functools.partial(image_kernel, chips, kept, together, chained, stored, scored),
        out_shape=shapes,
        grid=(heads,),
        in_specs=specs,
        out_specs=outs,
        scratch_shapes=[
            pltpu.VMEM((total + tile_rows, HD), queries.dtype),
            pltpu.VMEM((total + tile_rows, 2 * HD), queries.dtype),
            pltpu.VMEM((8, HD), jnp.float32),
            pltpu.SMEM((2 * chips,), jnp.int32),
        ],
        input_output_aliases=aliases,
        compiler_params=PARAMS,
        cost_estimate=lasting(2 * heads),
        name="attend_image" if stored else "last_rows",
    )(*operands)


def normalize_kernel(prompts, slots, every_ref, out_ref):
    own = lax.axis_index("prompt") * slots + lax.axis_index("slot")
    score = jnp.sum(every_ref[...], axis=1, keepdims=True)
    score = jnp.broadcast_to(score, every_ref.shape).reshape(prompts, slots, HD)
    deviation = score - jnp.sum(score, axis=1, keepdims=True) / slots
    spread = jnp.sum(jnp.sum(deviation * deviation, axis=0), axis=0, keepdims=True)
    advantage = deviation / jnp.sqrt(spread / (prompts * slots) + 1e-06)
    advantage = advantage.reshape(prompts * slots, HD)
    row = lax.broadcasted_iota(jnp.int32, advantage.shape, 0)
    out_ref[...] = jnp.sum(jnp.where(row == own, advantage, 0.0), axis=0, keepdims=True)[:, :1]


def per_device(patch_kv, routes, prefix_kv, prefix_len, queries, suffix_kv, score_head):
    slot_count = lax.axis_size("slot")
    prompt_count = lax.axis_size("prompt")
    chips = slot_count // 2
    kept = slot_count // 2
    me = lax.axis_index("slot").astype(jnp.int32).reshape(1)

    def swap(x, k):
        return lax.ppermute(x, "slot", [(i, i ^ k) for i in range(slot_count)])

    mate_patch, mate_routes = swap(patch_kv[0], 1), swap(routes[0], 1)
    near = [prefix_kv] + [swap(prefix_kv, 2 * offset) for offset in range(1, chips)]
    buffers = pack(PARTS, chips, me, routes[0], mate_routes, patch_kv[0], mate_patch)
    buffers = lax.optimization_barrier((list(buffers), near))[0]
    near = jnp.concatenate(near, axis=0)
    far = swap(near, 1)
    text = attend_text(me, prefix_len, queries[0, 0], near, far, suffix_kv[0, 0])

    head = score_head.reshape(1, -1)
    groups = [[2 * a + b for a in range(chips)] for b in range(2)]
    arrived, first = [], 0
    for n, (_, _, together) in enumerate(PARTS):
        sent = buffers[first : first + (1 if together else chips)]
        first += len(sent)
        if together:
            arrived.append(
                [lax.all_to_all(sent[0], "slot", 0, 0, tiled=True, axis_index_groups=groups)]
            )
        else:
            arrived.append(
                [sent[0]] + [swap(sent[offset], 2 * offset) for offset in range(1, chips)]
            )
    devices = prompt_count * slot_count
    image = functools.partial(attend_image, chips, kept)
    context, share = image(PARTS[0], head, queries[0, 0], text, arrived[0])
    (shares,) = image(
        PARTS[1], head, queries[0, 0], text, arrived[1], share=share, devices=devices
    )
    every = lax.all_to_all(shares, ("prompt", "slot"), 0, 0, tiled=True)
    (context,) = image(
        PARTS[1], head, queries[0, 0], text, arrived[1], context=context
    )
    advantage = pl.pallas_call(
        functools.partial(normalize_kernel, prompt_count, slot_count),
        out_shape=jax.ShapeDtypeStruct((1, 1), jnp.float32),
        in_specs=[pl.BlockSpec(memory_space=pltpu.VMEM)],
        out_specs=pl.BlockSpec(memory_space=pltpu.VMEM),
        cost_estimate=lasting(1),
        name="normalize",
    )(every)
    return (context[None, None], advantage)


def solution(mesh):
    placed = (
        P("prompt", "slot", None, None),
        P("prompt", "slot"),
        P("prompt", None, "slot"),
        P("prompt"),
        P("prompt", "slot", None, None),
        P("prompt", "slot", None, None),
        P(),
    )
    return jax.shard_map(
        per_device,
        mesh=mesh,
        in_specs=placed,
        out_specs=(P("prompt", "slot", None, None), P("prompt", "slot")),
        check_vma=False,
    )
```

```python
import functools
import math

import jax
import jax.numpy as jnp
from jax import lax
from jax.experimental import pallas as pl
from jax.experimental.pallas import tpu as pltpu
from jax.sharding import PartitionSpec as P

HEADS = 64
KVH = 8
HD = 128
GROUPS = HEADS // KVH
SCALE = math.log2(math.e) / math.sqrt(HD)
LOW = -1e30
ROOM = 100.0
PARTS = ((0, 5, False), (5, 3, False))
LAST = 16
EMPTY = 1024.0
NT = (((1,), (1,)), ((), ()))


def lasting(microseconds):
    return pl.CostEstimate(flops=0, bytes_accessed=int(microseconds * 3.5e6), transcendentals=0)


PARAMS = pltpu.CompilerParams(vmem_limit_bytes=62 * 2**20)


def slot_of(judge, routes):
    tile, found = jnp.int32(0), jnp.bool_(False)
    for s in range(routes.shape[0]):
        here = routes[s] == judge
        tile, found = jnp.where(here, s, tile), found | here
    return tile, found


def pack_kernel(chips, parts, me, routes, mate_routes, *rest):
    tiles, outs = rest[: 2 * chips], list(rest[2 * chips :])
    chip, core = me[0] // 2, me[0] % 2
    top = (lax.broadcasted_iota(jnp.int32, (16, HD), 0) == 0) & (pl.program_id(0) == 0)
    for head_from, heads, together in parts:
        width = heads * HD
        for offset in range(chips):
            out = outs[0].at[chip ^ offset] if together else outs.pop(0)
            for n, held in enumerate((routes, mate_routes)):
                tile = tiles[2 * offset + n]
                found = slot_of(2 * (chip ^ offset) + core, held)[1]
                for half in range(2):
                    first = (half * KVH + head_from) * HD
                    out[n, :, half * width : (half + 1) * width] = tile[0, :, first : first + width]
                mark = top & jnp.logical_not(found)
                kept = tile[0, :16, head_from * HD : (head_from + 1) * HD]
                out[n, :16, :HD] = jnp.where(mark, jnp.full_like(kept, EMPTY), kept)
        if together:
            outs.pop(0)


def pack(parts, chips, me, routes, mate_routes, patch, mate_patch):
    tile_rows, width = patch.shape[1:]
    rows = tile_rows // 4
    shapes, specs, sources = [], [], []
    for _, heads, together in parts:
        shape = (2, tile_rows, 2 * heads * HD)
        block = (2, rows, 2 * heads * HD)
        if together:
            shapes.append((chips,) + shape)
            specs.append(pl.BlockSpec((chips,) + block, lambda r, *_: (0, 0, r, 0)))
        else:
            shapes += [shape] * chips
            specs += [pl.BlockSpec(block, lambda r, *_: (0, r, 0))] * chips
    for offset in range(chips):
        for n in range(2):

            def source(r, me, *held, offset=offset, n=n):
                judge = 2 * ((me[0] // 2) ^ offset) + me[0] % 2
                return slot_of(judge, held[n])[0], r, 0

            sources.append(pl.BlockSpec((1, rows, width), source))
    return pl.pallas_call(
        functools.partial(pack_kernel, chips, parts),
        out_shape=[jax.ShapeDtypeStruct(shape, patch.dtype) for shape in shapes],
        grid_spec=pltpu.PrefetchScalarGridSpec(
            num_scalar_prefetch=3,
            grid=(tile_rows // rows,),
            in_specs=sources,
            out_specs=specs,
        ),
        compiler_params=PARAMS,
        cost_estimate=lasting(5),
        name="pack_tiles",
    )(me, routes, mate_routes, *([patch, mate_patch] * chips))


def pipelined(scores, finish):
    held = scores(0)
    for h in range(1, GROUPS):
        following = scores(h)
        finish(held, h - 1)
        held = following
    finish(held, GROUPS - 1)


def fill_text(me, length, head, blocks, sk_ref, sv_ref, kbuf, vbuf):
    prefix_rows, columns = blocks[0].shape
    chip, core = me[0] // 2, me[0] % 2
    live = lax.broadcasted_iota(jnp.int32, (prefix_rows, HD), 0) < length[0]
    for buf, column, ref in ((kbuf, head, sk_ref), (vbuf, KVH + head, sv_ref)):
        owner, within = column // (columns // HD), column % (columns // HD)
        wanted = 2 * ((owner // 2) ^ chip) + ((owner % 2) ^ core)
        span = pl.ds(pl.multiple_of(within * HD, HD), HD)
        for n, block in enumerate(blocks):

            @pl.when(wanted == n)
            def _(buf=buf, block=block, span=span):
                rows = block[:, span]
                other = rows[0:1, :] if buf is kbuf else jnp.zeros_like(rows)
                buf[:prefix_rows, :HD] = jnp.where(live, rows, other)

        buf[prefix_rows:, :HD] = ref[...]

    @pl.when(pl.program_id(0) == 0)
    def _():
        vbuf[:prefix_rows, HD:] = live.astype(vbuf.dtype)
        vbuf[prefix_rows:, HD:] = jnp.ones((sk_ref.shape[0], HD), vbuf.dtype)


def text_kernel(slots, me, length, q_ref, *rest):
    blocks, (sk_ref, sv_ref, o_ref, stat_ref, kv_ref, kbuf, vbuf) = rest[:slots], rest[slots:]
    suffix_rows = sk_ref.shape[0]
    prefix_rows = kbuf.shape[0] - suffix_rows
    fill_text(me, length, pl.program_id(0), blocks, sk_ref, sv_ref, kbuf, vbuf)
    kv_ref[0, :, :HD] = kbuf[...]
    kv_ref[0, :, HD:] = vbuf[:, :HD]
    causal = lax.broadcasted_iota(jnp.int32, (suffix_rows, suffix_rows), 1) <= lax.broadcasted_iota(
        jnp.int32, (suffix_rows, suffix_rows), 0
    )

    def scores(h):
        s = lax.dot_general(
            q_ref[:, h * HD : (h + 1) * HD], kbuf[...], NT, preferred_element_type=jnp.float32
        )
        return jnp.concatenate(
            [s[:, :prefix_rows], jnp.where(causal, s[:, prefix_rows:], LOW)], axis=1
        )

    def finish(s, h):
        peak = jnp.max(s, axis=1, keepdims=True)
        weights = jnp.exp2((s - peak) * SCALE).astype(jnp.bfloat16)
        mixed = jnp.dot(weights, vbuf[...], preferred_element_type=jnp.float32)
        o_ref[:, h * HD : (h + 1) * HD] = mixed[:, :HD]
        stat_ref[:, h : h + 1] = peak
        stat_ref[:, GROUPS + h : GROUPS + h + 1] = mixed[:, HD : HD + 1]

    pipelined(scores, finish)


def attend_text(me, length, queries, prefix, suffix):
    rows = queries.shape[0]
    total, wide = prefix[0].shape[0] + suffix.shape[0], GROUPS * HD
    column = lambda g, *_: (0, g)
    return pl.pallas_call(
        functools.partial(text_kernel, len(prefix)),
        out_shape=[
            jax.ShapeDtypeStruct(queries.shape, jnp.float32),
            jax.ShapeDtypeStruct((rows, KVH * HD), jnp.float32),
            jax.ShapeDtypeStruct((KVH, total, 2 * HD), queries.dtype),
        ],
        grid_spec=pltpu.PrefetchScalarGridSpec(
            num_scalar_prefetch=2,
            grid=(KVH,),
            in_specs=[pl.BlockSpec((rows, wide), column)]
            + [pl.BlockSpec(block.shape, lambda g, *_: (0, 0)) for block in prefix]
            + [
                pl.BlockSpec((suffix.shape[0], HD), column),
                pl.BlockSpec((suffix.shape[0], HD), lambda g, *_: (0, KVH + g)),
            ],
            out_specs=[
                pl.BlockSpec((rows, wide), column),
                pl.BlockSpec((rows, HD), column),
                pl.BlockSpec((1, total, 2 * HD), lambda g, *_: (g, 0, 0)),
            ],
            scratch_shapes=[
                pltpu.VMEM((total, HD), queries.dtype),
                pltpu.VMEM((total, 2 * HD), queries.dtype),
            ],
        ),
        compiler_params=PARAMS,
        cost_estimate=lasting(21),
        name="attend_text",
    )(me, length, queries, *prefix, suffix, suffix)


def tile_at(tiles, n):
    return tiles[0].at[n // 2, n % 2] if len(tiles) == 1 else tiles[n // 2].at[n % 2]


def place_tiles(slots, kept, tiles, place_ref):
    count = jnp.int32(0)
    for n in range(slots):
        found = jnp.max(tile_at(tiles, n)[0:1, :HD].astype(jnp.float32)) < EMPTY
        place_ref[n] = jnp.where(found, count, kept)
        count = count + jnp.where(found, 1, 0)


def fill_image(slots, head, tiles, place_ref, kbuf, vbuf):
    tile_rows, width = tiles[0].shape[-2], tiles[0].shape[-1] // 2
    for n in range(slots):
        row = pl.ds(pl.multiple_of(place_ref[n] * tile_rows, tile_rows), tile_rows)
        tile = tile_at(tiles, n)
        for buf, first in ((kbuf, 0), (vbuf, width)):
            column = first + head * HD
            column = column if isinstance(head, int) else pl.multiple_of(column, HD)
            buf[row, :HD] = tile[:, pl.ds(column, HD)]


def image_kernel(slots, kept, count, last, q_ref, acc_ref, stat_ref, *rest):
    tiles, rest = rest[:count], rest[count:]
    if last:
        length, last_ref, head_ref, text_ref, o_ref, score_ref, kbuf, vbuf, place_ref = rest[:9]
        last_kbuf, last_vbuf, kv_ref, sem = rest[9:]
        head_from, heads, prefix_rows = last
        copy = pltpu.make_async_copy(text_ref.at[pl.ds(head_from, heads)], kv_ref, sem)
    else:
        o_ref, kbuf, vbuf, place_ref = rest[-4:]
    tile_rows = tiles[0].shape[-2]
    total, rows = kept * tile_rows, q_ref.shape[0]
    g = pl.program_id(0)

    @pl.when(g == 0)
    def _():
        vbuf[:, HD:] = jnp.ones((total + tile_rows, HD), vbuf.dtype)
        place_tiles(slots, kept, tiles, place_ref)
        if last:
            copy.start()

    fill_image(slots, g, tiles, place_ref, kbuf, vbuf)

    def scores(column):
        return lax.dot_general(
            q_ref[:, column], kbuf[:total], NT, preferred_element_type=jnp.float32
        )

    def close(summed, totals, column):
        o_ref[:, column] = (summed / totals).astype(o_ref.dtype)

    largest = [jnp.full((8, HD), LOW, jnp.float32)]

    def finish(s, h):
        column = slice(h * HD, (h + 1) * HD)
        held = stat_ref[:, h : h + 1]
        powers = []
        for k in range(total // HD):
            power = (s[:, k * HD : (k + 1) * HD] - held) * SCALE
            largest[0] = jnp.maximum(largest[0], jnp.max(power.reshape(rows // 8, 8, HD), axis=0))
            powers.append(jnp.exp2(power).astype(jnp.bfloat16))
        weights = jnp.concatenate(powers, axis=1)
        mixed = jnp.dot(weights, vbuf[:total], preferred_element_type=jnp.float32)
        totals = mixed[:, HD:] + stat_ref[:, GROUPS + h : GROUPS + h + 1]
        close(mixed[:, :HD] + acc_ref[:, column], totals, column)

    pipelined(lambda h: scores(slice(h * HD, (h + 1) * HD)), finish)

    @pl.when(jnp.logical_not(jnp.max(largest[0]) < ROOM))
    def _():
        @pl.loop(0, GROUPS)
        def _(h):
            column = pl.ds(pl.multiple_of(h * HD, HD), HD)
            s = scores(column)
            lane = lax.broadcasted_iota(jnp.int32, (rows, HD), 1)
            held = jnp.sum(jnp.where(lane == h, stat_ref[...], 0.0), axis=1, keepdims=True)
            sums = jnp.where(lane == GROUPS + h, stat_ref[...], 0.0)
            sums = jnp.sum(sums, axis=1, keepdims=True)
            peak = jnp.maximum(held, jnp.max(s, axis=1, keepdims=True))
            weights = jnp.exp2((s - peak) * SCALE).astype(jnp.bfloat16)
            mixed = jnp.dot(weights, vbuf[:total], preferred_element_type=jnp.float32)
            fade = jnp.exp2((held - peak) * SCALE)
            summed = acc_ref[:, column] * fade + mixed[:, :HD]
            close(summed, sums * fade + mixed[:, HD:], column)

    if last:
        @pl.when(g == heads - 1)
        def _():
            copy.wait()
            score_ref[...] = last_row_gain(
                slots, head_from, heads, prefix_rows, total, length, last_ref, head_ref, kv_ref, tiles,
                place_ref, last_kbuf, last_vbuf,
            )


def attend_image(chips, kept, part, tiles, queries, summed, stats, context=None, last=None):
    head_from, heads, _ = part
    tile_rows = tiles[0].shape[-2]
    total, wide, rows = kept * tile_rows, GROUPS * HD, queries.shape[0]
    column = lambda g: (0, head_from + g)
    specs = [pl.BlockSpec((rows, wide), column)] * 2 + [pl.BlockSpec((rows, HD), column)]
    specs += [pl.BlockSpec(tile.shape, lambda g, d=tile.ndim: (0,) * d) for tile in tiles]
    operands = [queries, summed, stats, *tiles]
    shapes = [jax.ShapeDtypeStruct(queries.shape, queries.dtype)]
    outs = [pl.BlockSpec((rows, wide), column)]
    scratch = [
        pltpu.VMEM((total + tile_rows, HD), queries.dtype),
        pltpu.VMEM((total + tile_rows, 2 * HD), queries.dtype),
        pltpu.SMEM((2 * chips,), jnp.int32),
    ]
    aliases, static = {}, None
    if last is not None:
        length, prefix_rows, head, text_rows = last
        static = (head_from, heads, prefix_rows)
        end = rows // LAST - 1
        operands += [length, queries, head, text_rows]
        specs += [
            pl.BlockSpec(memory_space=pltpu.SMEM),
            pl.BlockSpec((LAST, queries.shape[1]), lambda g: (end, 0)),
            pl.BlockSpec(head.shape, lambda g: (0, 0)),
            pl.BlockSpec(memory_space=pl.ANY),
        ]
        shapes.append(jax.ShapeDtypeStruct((GROUPS, HD), jnp.float32))
        outs.append(pl.BlockSpec((GROUPS, HD), lambda g: (0, 0)))
        scratch += last_scratch(heads, total + tile_rows, queries.dtype) + [
            pltpu.VMEM((heads,) + text_rows.shape[1:], queries.dtype),
            pltpu.SemaphoreType.DMA,
        ]
    if context is not None:
        aliases = {len(operands): 0}
        operands.append(context)
        specs.append(pl.BlockSpec(memory_space=pl.ANY))
    return pl.pallas_call(
        functools.partial(image_kernel, 2 * chips, kept, len(tiles), static),
        out_shape=shapes,
        grid=(heads,),
        in_specs=specs,
        out_specs=outs,
        scratch_shapes=scratch,
        input_output_aliases=aliases,
        compiler_params=PARAMS,
        cost_estimate=lasting(2 * heads),
        name="attend_image",
    )(*operands)


def last_row_gain(slots, head_from, heads, prefix_rows, total, length, q_ref, head_ref, kv_ref, tiles, place_ref, kbuf, vbuf):
    gain = jnp.zeros((GROUPS, HD), jnp.float32)
    column = lax.broadcasted_iota(jnp.int32, (GROUPS, kv_ref.shape[1]), 1)
    live = (column < length[0]) | (column >= prefix_rows)
    for i in range(heads):
        fill_image(slots, i, tiles, place_ref, kbuf.at[i], vbuf.at[i])
    for i in range(heads):
        first = (head_from + i) * GROUPS
        q = [q_ref[:, (first + h) * HD : (first + h + 1) * HD] for h in range(GROUPS)]
        q = jnp.concatenate([part.astype(jnp.float32)[-1:] for part in q], axis=0)
        q = q.astype(jnp.bfloat16)
        s = [
            lax.dot_general(q, keys, NT, preferred_element_type=jnp.float32)
            for keys in (kv_ref[i, :, :HD], kbuf[i, :total])
        ]
        s[0] = jnp.where(live, s[0], LOW)
        peak = jnp.maximum(*[jnp.max(part, axis=1, keepdims=True) for part in s])
        weights = [jnp.exp2((part - peak) * SCALE) for part in s]
        mixed = sum(
            jnp.dot(part.astype(jnp.bfloat16), values, preferred_element_type=jnp.float32)
            for part, values in zip(weights, (kv_ref[i, :, HD:], vbuf[i, :total]))
        )
        totals = sum(jnp.sum(part, axis=1, keepdims=True) for part in weights)
        out = (mixed / totals).astype(jnp.bfloat16).astype(jnp.float32)
        gain = gain + out * head_ref[first : first + GROUPS, :]
    return gain


def last_kernel(slots, kept, count, head_from, heads, prefix_rows, length, q_ref, head_ref, kv_ref, *rest):
    tiles, (before, score_ref, kbuf, vbuf, place_ref) = rest[:count], rest[count:]
    total = kept * tiles[0].shape[-2]
    place_tiles(slots, kept, tiles, place_ref)
    gain = before[...] + last_row_gain(
        slots, head_from, heads, prefix_rows, total, length, q_ref, head_ref, kv_ref, tiles, place_ref,
        kbuf, vbuf,
    )
    score_ref[...] = jnp.broadcast_to(jnp.sum(gain, axis=0, keepdims=True), score_ref.shape)


def last_scratch(heads, rows, dtype):
    return [pltpu.VMEM((heads, rows, HD), dtype)] * 2


def last_rows(chips, kept, part, tiles, queries, length, prefix_rows, head, text_rows, share, devices):
    head_from, heads, _ = part
    tile_rows, text = tiles[0].shape[-2], text_rows.shape[1]
    whole = lambda x: pl.BlockSpec(x.shape, lambda g, d=x.ndim: (0,) * d)
    end = queries.shape[0] // LAST - 1
    specs = [
        pl.BlockSpec(memory_space=pltpu.SMEM),
        pl.BlockSpec((LAST, queries.shape[1]), lambda g: (end, 0)),
        whole(head),
        pl.BlockSpec(
            (pl.Element(heads), pl.Element(text), pl.Element(2 * HD)), lambda g: (head_from, 0, 0)
        ),
    ]
    shape = (devices, HD)
    return pl.pallas_call(
        functools.partial(
            last_kernel, 2 * chips, kept, len(tiles), head_from, heads, prefix_rows
        ),
        out_shape=jax.ShapeDtypeStruct(shape, jnp.float32),
        grid=(1,),
        in_specs=specs + [whole(tile) for tile in tiles] + [whole(share)],
        out_specs=pl.BlockSpec(shape, lambda g: (0, 0)),
        scratch_shapes=last_scratch(heads, (kept + 1) * tile_rows, queries.dtype)
        + [pltpu.SMEM((2 * chips,), jnp.int32)],
        compiler_params=PARAMS,
        cost_estimate=lasting(heads),
        name="last_rows",
    )(length, queries, head, text_rows, *tiles, share)


def normalize_kernel(prompts, slots, every_ref, out_ref):
    own = lax.axis_index("prompt") * slots + lax.axis_index("slot")
    score = jnp.sum(every_ref[...], axis=1, keepdims=True)
    score = jnp.broadcast_to(score, every_ref.shape).reshape(prompts, slots, HD)
    deviation = score - jnp.sum(score, axis=1, keepdims=True) / slots
    spread = jnp.sum(jnp.sum(deviation * deviation, axis=0), axis=0, keepdims=True)
    advantage = deviation / jnp.sqrt(spread / (prompts * slots) + 1e-06)
    advantage = advantage.reshape(prompts * slots, HD)
    row = lax.broadcasted_iota(jnp.int32, advantage.shape, 0)
    out_ref[...] = jnp.sum(jnp.where(row == own, advantage, 0.0), axis=0, keepdims=True)[:, :1]


def per_device(patch_kv, routes, prefix_kv, prefix_len, queries, suffix_kv, score_head):
    slot_count = lax.axis_size("slot")
    prompt_count = lax.axis_size("prompt")
    chips = slot_count // 2
    kept = slot_count // 2
    me = lax.axis_index("slot").astype(jnp.int32).reshape(1)

    def swap(x, k):
        return lax.ppermute(x, "slot", [(i, i ^ k) for i in range(slot_count)])

    mate_patch, mate_routes = swap(patch_kv[0], 1), swap(routes[0], 1)
    near = [prefix_kv[0]] + [swap(prefix_kv[0], 2 * offset) for offset in range(1, chips)]
    buffers = pack(PARTS, chips, me, routes[0], mate_routes, patch_kv[0], mate_patch)
    held = lax.optimization_barrier((near[1:], buffers[0]))[0]
    far = [swap(block, 1) for block in [near[0], *held]]
    first = lax.optimization_barrier((buffers[:chips], near[:-1]))[0]
    prefix = [block for pair in zip(near, far) for block in pair]
    suffix = suffix_kv[0, 0]
    summed, stats, text_rows = attend_text(me, prefix_len, queries[0, 0], prefix, suffix)

    second = lax.optimization_barrier((buffers[chips:], stats))[0]
    arrived = [
        [sent[0]] + [swap(sent[offset], 2 * offset) for offset in range(1, chips)]
        for sent in (first, second)
    ]
    head = score_head.reshape(HEADS, HD)
    last = (prefix_len, prefix_kv.shape[1], head, text_rows)
    main = (queries[0, 0], summed, stats)
    context, share = attend_image(chips, kept, PARTS[0], arrived[0], *main, last=last)
    devices = prompt_count * slot_count
    shares = last_rows(chips, kept, PARTS[1], arrived[1], queries[0, 0], *last, share, devices)
    every = lax.all_to_all(shares, ("prompt", "slot"), 0, 0, tiled=True)
    (context,) = attend_image(chips, kept, PARTS[1], arrived[1], *main, context)
    advantage = pl.pallas_call(
        functools.partial(normalize_kernel, prompt_count, slot_count),
        out_shape=jax.ShapeDtypeStruct((1, 1), jnp.float32),
        in_specs=[pl.BlockSpec(memory_space=pltpu.VMEM)],
        out_specs=pl.BlockSpec(memory_space=pltpu.VMEM),
        cost_estimate=lasting(1),
        name="normalize",
    )(every)
    return (context[None, None], advantage)


def solution(mesh):
    placed = (
        P("prompt", "slot", None, None),
        P("prompt", "slot"),
        P("prompt", None, "slot"),
        P("prompt"),
        P("prompt", "slot", None, None),
        P("prompt", "slot", None, None),
        P(),
    )
    return jax.shard_map(
        per_device,
        mesh=mesh,
        in_specs=placed,
        out_specs=(P("prompt", "slot", None, None), P("prompt", "slot")),
        check_vma=False,
    )
```

```python
import functools
import math

import jax
import jax.numpy as jnp
from jax import lax
from jax.experimental import pallas as pl
from jax.experimental.pallas import tpu as pltpu
from jax.sharding import PartitionSpec as P

HEADS = 64
KVH = 8
HD = 128
GROUPS = HEADS // KVH
SCALE = math.log2(math.e) / math.sqrt(HD)
LOW = -1e30
ROOM = 2.0**100
PARTS = ((0, 5, False), (5, 3, False))
LAST = 16
EMPTY = 1024.0
NT = (((1,), (1,)), ((), ()))


def lasting(microseconds):
    return pl.CostEstimate(flops=0, bytes_accessed=int(microseconds * 3.5e6), transcendentals=0)


PARAMS = pltpu.CompilerParams(vmem_limit_bytes=64 * 2**20)


def slot_of(judge, routes):
    tile, found = jnp.int32(0), jnp.bool_(False)
    for s in range(routes.shape[0]):
        here = routes[s] == judge
        tile, found = jnp.where(here, s, tile), found | here
    return tile, found


def pack_kernel(chips, parts, me, routes, mate_routes, *rest):
    tiles, outs = rest[: 2 * chips], list(rest[2 * chips :])
    chip, core = me[0] // 2, me[0] % 2
    top = (lax.broadcasted_iota(jnp.int32, (16, HD), 0) == 0) & (pl.program_id(0) == 0)
    for head_from, heads, together in parts:
        width = heads * HD
        for offset in range(chips):
            out = outs[0].at[chip ^ offset] if together else outs.pop(0)
            for n, held in enumerate((routes, mate_routes)):
                tile = tiles[2 * offset + n]
                found = slot_of(2 * (chip ^ offset) + core, held)[1]
                for half in range(2):
                    first = (half * KVH + head_from) * HD
                    out[n, :, half * width : (half + 1) * width] = tile[0, :, first : first + width]
                mark = top & jnp.logical_not(found)
                kept = tile[0, :16, head_from * HD : (head_from + 1) * HD]
                out[n, :16, :HD] = jnp.where(mark, jnp.full_like(kept, EMPTY), kept)
        if together:
            outs.pop(0)


def pack(parts, chips, me, routes, mate_routes, patch, mate_patch):
    tile_rows, width = patch.shape[1:]
    rows = tile_rows // 4
    shapes, specs, sources = [], [], []
    for _, heads, together in parts:
        shape = (2, tile_rows, 2 * heads * HD)
        block = (2, rows, 2 * heads * HD)
        if together:
            shapes.append((chips,) + shape)
            specs.append(pl.BlockSpec((chips,) + block, lambda r, *_: (0, 0, r, 0)))
        else:
            shapes += [shape] * chips
            specs += [pl.BlockSpec(block, lambda r, *_: (0, r, 0))] * chips
    for offset in range(chips):
        for n in range(2):

            def source(r, me, *held, offset=offset, n=n):
                judge = 2 * ((me[0] // 2) ^ offset) + me[0] % 2
                return slot_of(judge, held[n])[0], r, 0

            sources.append(pl.BlockSpec((1, rows, width), source))
    return pl.pallas_call(
        functools.partial(pack_kernel, chips, parts),
        out_shape=[jax.ShapeDtypeStruct(shape, patch.dtype) for shape in shapes],
        grid_spec=pltpu.PrefetchScalarGridSpec(
            num_scalar_prefetch=3,
            grid=(tile_rows // rows,),
            in_specs=sources,
            out_specs=specs,
        ),
        compiler_params=PARAMS,
        cost_estimate=lasting(5),
        name="pack_tiles",
    )(me, routes, mate_routes, *([patch, mate_patch] * chips))


def pipelined(scores, finish):
    held = scores(0)
    for h in range(1, GROUPS):
        following = scores(h)
        finish(held, h - 1)
        held = following
    finish(held, GROUPS - 1)


def fill_text(me, length, head, blocks, sk_ref, sv_ref, held, kbuf, vbuf):
    prefix_rows, columns = blocks[0].shape
    live = lax.broadcasted_iota(jnp.int32, (prefix_rows, HD), 0) < length[0]

    @pl.when(pl.program_id(0) == 0)
    def _():
        chip, core = me[0] // 2, me[0] % 2
        for n, block in enumerate(blocks):
            held[2 * (chip ^ (n // 2)) + (core ^ (n % 2))] = block[...]
        vbuf[:prefix_rows, HD:] = live.astype(vbuf.dtype)
        vbuf[prefix_rows:, HD:] = jnp.ones((sk_ref.shape[0], HD), vbuf.dtype)

    for buf, column, ref in ((kbuf, head, sk_ref), (vbuf, KVH + head, sv_ref)):
        owner, within = column // (columns // HD), column % (columns // HD)
        rows = held[owner, :, pl.ds(pl.multiple_of(within * HD, HD), HD)]
        other = rows[0:1, :] if buf is kbuf else jnp.zeros_like(rows)
        buf[:prefix_rows, :HD] = jnp.where(live, rows, other)
        buf[prefix_rows:, :HD] = ref[...]


def text_kernel(slots, me, length, q_ref, *rest):
    blocks, (sk_ref, sv_ref, o_ref, stat_ref, kv_ref, held, kbuf, vbuf) = rest[:slots], rest[slots:]
    suffix_rows = sk_ref.shape[0]
    prefix_rows = kbuf.shape[0] - suffix_rows
    fill_text(me, length, pl.program_id(0), blocks, sk_ref, sv_ref, held, kbuf, vbuf)
    kv_ref[0, :, :HD] = kbuf[...]
    kv_ref[0, :, HD:] = vbuf[:, :HD]
    causal = lax.broadcasted_iota(jnp.int32, (suffix_rows, suffix_rows), 1) <= lax.broadcasted_iota(
        jnp.int32, (suffix_rows, suffix_rows), 0
    )

    lane = lax.broadcasted_iota(jnp.int32, (suffix_rows, HD), 1)

    def scores(h):
        s = lax.dot_general(
            q_ref[:, h * HD : (h + 1) * HD], kbuf[...], NT, preferred_element_type=jnp.float32
        )
        return jnp.concatenate(
            [s[:, :prefix_rows], jnp.where(causal, s[:, prefix_rows:], LOW)], axis=1
        )

    def finish(s, h):
        peak = jnp.max(s, axis=1, keepdims=True)
        weights = jnp.exp2((s - peak) * SCALE).astype(jnp.bfloat16)
        mixed = jnp.dot(weights, vbuf[...], preferred_element_type=jnp.float32)
        o_ref[:, h * HD : (h + 1) * HD] = mixed[:, :HD]
        held = jnp.where(lane == GROUPS + h, mixed[:, HD:], stat_ref[...])
        stat_ref[...] = jnp.where(lane == h, peak, held)

    pipelined(scores, finish)


def attend_text(me, length, queries, prefix, suffix):
    rows = queries.shape[0]
    total, wide = prefix[0].shape[0] + suffix.shape[0], GROUPS * HD
    column = lambda g, *_: (0, g)
    return pl.pallas_call(
        functools.partial(text_kernel, len(prefix)),
        out_shape=[
            jax.ShapeDtypeStruct(queries.shape, jnp.float32),
            jax.ShapeDtypeStruct((rows, KVH * HD), jnp.float32),
            jax.ShapeDtypeStruct((KVH, total, 2 * HD), queries.dtype),
        ],
        grid_spec=pltpu.PrefetchScalarGridSpec(
            num_scalar_prefetch=2,
            grid=(KVH,),
            in_specs=[pl.BlockSpec((rows, wide), column)]
            + [pl.BlockSpec(block.shape, lambda g, *_: (0, 0)) for block in prefix]
            + [
                pl.BlockSpec((suffix.shape[0], HD), column),
                pl.BlockSpec((suffix.shape[0], HD), lambda g, *_: (0, KVH + g)),
            ],
            out_specs=[
                pl.BlockSpec((rows, wide), column),
                pl.BlockSpec((rows, HD), column),
                pl.BlockSpec((1, total, 2 * HD), lambda g, *_: (g, 0, 0)),
            ],
            scratch_shapes=[
                pltpu.VMEM((len(prefix),) + prefix[0].shape, queries.dtype),
                pltpu.VMEM((total, HD), queries.dtype),
                pltpu.VMEM((total, 2 * HD), queries.dtype),
            ],
        ),
        compiler_params=PARAMS,
        cost_estimate=lasting(21),
        name="attend_text",
    )(me, length, queries, *prefix, suffix, suffix)


def tile_at(tiles, n):
    return tiles[0].at[n // 2, n % 2] if len(tiles) == 1 else tiles[n // 2].at[n % 2]


def place_tiles(slots, kept, tiles, place_ref):
    count = jnp.int32(0)
    for n in range(slots):
        found = jnp.max(tile_at(tiles, n)[0:1, :HD].astype(jnp.float32)) < EMPTY
        place_ref[n] = jnp.where(found, count, kept)
        count = count + jnp.where(found, 1, 0)


def fill_image(slots, head, tiles, place_ref, kbuf, vbuf):
    tile_rows, width = tiles[0].shape[-2], tiles[0].shape[-1] // 2
    for n in range(slots):
        row = pl.ds(pl.multiple_of(place_ref[n] * tile_rows, tile_rows), tile_rows)
        tile = tile_at(tiles, n)
        for buf, first in ((kbuf, 0), (vbuf, width)):
            column = first + head * HD
            column = column if isinstance(head, int) else pl.multiple_of(column, HD)
            buf[row, :HD] = tile[:, pl.ds(column, HD)]


def image_kernel(slots, kept, count, last, q_ref, acc_ref, stat_ref, *rest):
    tiles, rest = rest[:count], rest[count:]
    if last:
        length, last_ref, head_ref, text_ref, o_ref, score_ref, kbuf, vbuf, place_ref = rest[:9]
        last_kbuf, last_vbuf, kv_ref, sem = rest[9:]
        head_from, heads, prefix_rows = last
        copy = pltpu.make_async_copy(text_ref.at[pl.ds(head_from, heads)], kv_ref, sem)
    else:
        o_ref, kbuf, vbuf, place_ref = rest[-4:]
    tile_rows = tiles[0].shape[-2]
    total, rows = kept * tile_rows, q_ref.shape[0]
    g = pl.program_id(0)

    @pl.when(g == 0)
    def _():
        vbuf[:, HD:] = jnp.ones((total + tile_rows, HD), vbuf.dtype)
        place_tiles(slots, kept, tiles, place_ref)
        if last:
            copy.start()

    fill_image(slots, g, tiles, place_ref, kbuf, vbuf)

    def scores(column):
        return lax.dot_general(
            q_ref[:, column], kbuf[:total], NT, preferred_element_type=jnp.float32
        )

    def close(summed, totals, column):
        o_ref[:, column] = (summed / totals).astype(o_ref.dtype)

    largest = [jnp.zeros((8, HD), jnp.float32)]

    def finish(s, h):
        column = slice(h * HD, (h + 1) * HD)
        held = stat_ref[:, h : h + 1]
        powers = []
        for k in range(total // HD):
            power = (s[:, k * HD : (k + 1) * HD] - held) * SCALE
            powers.append(jnp.exp2(power).astype(jnp.bfloat16))
        weights = jnp.concatenate(powers, axis=1)
        mixed = jnp.dot(weights, vbuf[:total], preferred_element_type=jnp.float32)
        totals = mixed[:, HD:] + stat_ref[:, GROUPS + h : GROUPS + h + 1]
        largest[0] = jnp.maximum(largest[0], jnp.max(totals.reshape(rows // 8, 8, HD), axis=0))
        close(mixed[:, :HD] + acc_ref[:, column], totals, column)

    pipelined(lambda h: scores(slice(h * HD, (h + 1) * HD)), finish)

    @pl.when(jnp.logical_not(jnp.max(largest[0]) < ROOM))
    def _():
        @pl.loop(0, GROUPS)
        def _(h):
            column = pl.ds(pl.multiple_of(h * HD, HD), HD)
            s = scores(column)
            lane = lax.broadcasted_iota(jnp.int32, (rows, HD), 1)
            held = jnp.sum(jnp.where(lane == h, stat_ref[...], 0.0), axis=1, keepdims=True)
            sums = jnp.where(lane == GROUPS + h, stat_ref[...], 0.0)
            sums = jnp.sum(sums, axis=1, keepdims=True)
            peak = jnp.maximum(held, jnp.max(s, axis=1, keepdims=True))
            weights = jnp.exp2((s - peak) * SCALE).astype(jnp.bfloat16)
            mixed = jnp.dot(weights, vbuf[:total], preferred_element_type=jnp.float32)
            fade = jnp.exp2((held - peak) * SCALE)
            summed = acc_ref[:, column] * fade + mixed[:, :HD]
            close(summed, sums * fade + mixed[:, HD:], column)

    if last:
        @pl.when(g == heads - 1)
        def _():
            copy.wait()
            score_ref[...] = last_row_gain(
                slots, head_from, heads, prefix_rows, total, length, last_ref, head_ref, kv_ref, tiles,
                place_ref, last_kbuf, last_vbuf,
            )


def attend_image(chips, kept, part, tiles, queries, summed, stats, context=None, last=None):
    head_from, heads, _ = part
    tile_rows = tiles[0].shape[-2]
    total, wide, rows = kept * tile_rows, GROUPS * HD, queries.shape[0]
    column = lambda g: (0, head_from + g)
    specs = [pl.BlockSpec((rows, wide), column)] * 2 + [pl.BlockSpec((rows, HD), column)]
    specs += [pl.BlockSpec(tile.shape, lambda g, d=tile.ndim: (0,) * d) for tile in tiles]
    operands = [queries, summed, stats, *tiles]
    shapes = [jax.ShapeDtypeStruct(queries.shape, queries.dtype)]
    outs = [pl.BlockSpec((rows, wide), column)]
    scratch = [
        pltpu.VMEM((total + tile_rows, HD), queries.dtype),
        pltpu.VMEM((total + tile_rows, 2 * HD), queries.dtype),
        pltpu.SMEM((2 * chips,), jnp.int32),
    ]
    aliases, static = {}, None
    if last is not None:
        length, prefix_rows, head, text_rows = last
        static = (head_from, heads, prefix_rows)
        end = rows // LAST - 1
        operands += [length, queries, head, text_rows]
        specs += [
            pl.BlockSpec(memory_space=pltpu.SMEM),
            pl.BlockSpec((LAST, queries.shape[1]), lambda g: (end, 0)),
            pl.BlockSpec(head.shape, lambda g: (0, 0)),
            pl.BlockSpec(memory_space=pl.ANY),
        ]
        shapes.append(jax.ShapeDtypeStruct((GROUPS, HD), jnp.float32))
        outs.append(pl.BlockSpec((GROUPS, HD), lambda g: (0, 0)))
        scratch += last_scratch(heads, total + tile_rows, queries.dtype) + [
            pltpu.VMEM((heads,) + text_rows.shape[1:], queries.dtype),
            pltpu.SemaphoreType.DMA,
        ]
    if context is not None:
        aliases = {len(operands): 0}
        operands.append(context)
        specs.append(pl.BlockSpec(memory_space=pl.ANY))
    return pl.pallas_call(
        functools.partial(image_kernel, 2 * chips, kept, len(tiles), static),
        out_shape=shapes,
        grid=(heads,),
        in_specs=specs,
        out_specs=outs,
        scratch_shapes=scratch,
        input_output_aliases=aliases,
        compiler_params=PARAMS,
        cost_estimate=lasting(2 * heads),
        name="attend_image",
    )(*operands)


def last_row_gain(slots, head_from, heads, prefix_rows, total, length, q_ref, head_ref, kv_ref, tiles, place_ref, kbuf, vbuf):
    gain = jnp.zeros((GROUPS, HD), jnp.float32)
    column = lax.broadcasted_iota(jnp.int32, (GROUPS, kv_ref.shape[1]), 1)
    live = (column < length[0]) | (column >= prefix_rows)
    for i in range(heads):
        fill_image(slots, i, tiles, place_ref, kbuf.at[i], vbuf.at[i])
    for i in range(heads):
        first = (head_from + i) * GROUPS
        q = [q_ref[:, (first + h) * HD : (first + h + 1) * HD] for h in range(GROUPS)]
        q = jnp.concatenate([part.astype(jnp.float32)[-1:] for part in q], axis=0)
        q = q.astype(jnp.bfloat16)
        s = [
            lax.dot_general(q, keys, NT, preferred_element_type=jnp.float32)
            for keys in (kv_ref[i, :, :HD], kbuf[i, :total])
        ]
        s[0] = jnp.where(live, s[0], LOW)
        peak = jnp.maximum(*[jnp.max(part, axis=1, keepdims=True) for part in s])
        weights = [jnp.exp2((part - peak) * SCALE) for part in s]
        mixed = sum(
            jnp.dot(part.astype(jnp.bfloat16), values, preferred_element_type=jnp.float32)
            for part, values in zip(weights, (kv_ref[i, :, HD:], vbuf[i, :total]))
        )
        totals = sum(jnp.sum(part, axis=1, keepdims=True) for part in weights)
        out = (mixed / totals).astype(jnp.bfloat16).astype(jnp.float32)
        gain = gain + out * head_ref[first : first + GROUPS, :]
    return gain


def last_kernel(slots, kept, count, head_from, heads, prefix_rows, length, q_ref, head_ref, kv_ref, *rest):
    tiles, (before, score_ref, kbuf, vbuf, place_ref) = rest[:count], rest[count:]
    total = kept * tiles[0].shape[-2]
    place_tiles(slots, kept, tiles, place_ref)
    gain = before[...] + last_row_gain(
        slots, head_from, heads, prefix_rows, total, length, q_ref, head_ref, kv_ref, tiles, place_ref,
        kbuf, vbuf,
    )
    score_ref[...] = jnp.broadcast_to(jnp.sum(gain, axis=0, keepdims=True), score_ref.shape)


def last_scratch(heads, rows, dtype):
    return [pltpu.VMEM((heads, rows, HD), dtype)] * 2


def last_rows(chips, kept, part, tiles, queries, length, prefix_rows, head, text_rows, share, devices):
    head_from, heads, _ = part
    tile_rows, text = tiles[0].shape[-2], text_rows.shape[1]
    whole = lambda x: pl.BlockSpec(x.shape, lambda g, d=x.ndim: (0,) * d)
    end = queries.shape[0] // LAST - 1
    specs = [
        pl.BlockSpec(memory_space=pltpu.SMEM),
        pl.BlockSpec((LAST, queries.shape[1]), lambda g: (end, 0)),
        whole(head),
        pl.BlockSpec(
            (pl.Element(heads), pl.Element(text), pl.Element(2 * HD)), lambda g: (head_from, 0, 0)
        ),
    ]
    shape = (devices, HD)
    return pl.pallas_call(
        functools.partial(
            last_kernel, 2 * chips, kept, len(tiles), head_from, heads, prefix_rows
        ),
        out_shape=jax.ShapeDtypeStruct(shape, jnp.float32),
        grid=(1,),
        in_specs=specs + [whole(tile) for tile in tiles] + [whole(share)],
        out_specs=pl.BlockSpec(shape, lambda g: (0, 0)),
        scratch_shapes=last_scratch(heads, (kept + 1) * tile_rows, queries.dtype)
        + [pltpu.SMEM((2 * chips,), jnp.int32)],
        compiler_params=PARAMS,
        cost_estimate=lasting(heads),
        name="last_rows",
    )(length, queries, head, text_rows, *tiles, share)


def normalize_kernel(prompts, slots, every_ref, out_ref):
    own = lax.axis_index("prompt") * slots + lax.axis_index("slot")
    score = jnp.sum(every_ref[...], axis=1, keepdims=True)
    score = jnp.broadcast_to(score, every_ref.shape).reshape(prompts, slots, HD)
    deviation = score - jnp.sum(score, axis=1, keepdims=True) / slots
    spread = jnp.sum(jnp.sum(deviation * deviation, axis=0), axis=0, keepdims=True)
    advantage = deviation / jnp.sqrt(spread / (prompts * slots) + 1e-06)
    advantage = advantage.reshape(prompts * slots, HD)
    row = lax.broadcasted_iota(jnp.int32, advantage.shape, 0)
    out_ref[...] = jnp.sum(jnp.where(row == own, advantage, 0.0), axis=0, keepdims=True)[:, :1]


def per_device(patch_kv, routes, prefix_kv, prefix_len, queries, suffix_kv, score_head):
    slot_count = lax.axis_size("slot")
    prompt_count = lax.axis_size("prompt")
    chips = slot_count // 2
    kept = slot_count // 2
    me = lax.axis_index("slot").astype(jnp.int32).reshape(1)

    def swap(x, k):
        return lax.ppermute(x, "slot", [(i, i ^ k) for i in range(slot_count)])

    mate_patch, mate_routes = swap(patch_kv[0], 1), swap(routes[0], 1)
    near = [prefix_kv[0]] + [swap(prefix_kv[0], 2 * offset) for offset in range(1, chips)]
    buffers = pack(PARTS, chips, me, routes[0], mate_routes, patch_kv[0], mate_patch)
    held = lax.optimization_barrier((near[1:], buffers[0]))[0]
    far = [swap(block, 1) for block in [near[0], *held]]
    first, second = list(buffers[:chips]), list(buffers[chips:])
    for n in range(1, chips):
        first[n] = lax.optimization_barrier((first[n], near[:-1] if n < chips - 1 else near))[0]
    prefix = [block for pair in zip(near, far) for block in pair]
    suffix = suffix_kv[0, 0]
    summed, stats, text_rows = attend_text(me, prefix_len, queries[0, 0], prefix, suffix)

    second[-1] = lax.optimization_barrier((second[-1], stats))[0]
    arrived = [
        [sent[0]] + [swap(sent[offset], 2 * offset) for offset in range(1, chips)]
        for sent in (first, second)
    ]
    head = score_head.reshape(HEADS, HD)
    last = (prefix_len, prefix_kv.shape[1], head, text_rows)
    main = (queries[0, 0], summed, stats)
    context, share = attend_image(chips, kept, PARTS[0], arrived[0], *main, last=last)
    devices = prompt_count * slot_count
    shares = last_rows(chips, kept, PARTS[1], arrived[1], queries[0, 0], *last, share, devices)
    every = lax.all_to_all(shares, ("prompt", "slot"), 0, 0, tiled=True)
    (context,) = attend_image(chips, kept, PARTS[1], arrived[1], *main, context)
    advantage = pl.pallas_call(
        functools.partial(normalize_kernel, prompt_count, slot_count),
        out_shape=jax.ShapeDtypeStruct((1, 1), jnp.float32),
        in_specs=[pl.BlockSpec(memory_space=pltpu.VMEM)],
        out_specs=pl.BlockSpec(memory_space=pltpu.VMEM),
        cost_estimate=lasting(1),
        name="normalize",
    )(every)
    return (context[None, None], advantage)


def solution(mesh):
    placed = (
        P("prompt", "slot", None, None),
        P("prompt", "slot"),
        P("prompt", None, "slot"),
        P("prompt"),
        P("prompt", "slot", None, None),
        P("prompt", "slot", None, None),
        P(),
    )
    return jax.shard_map(
        per_device,
        mesh=mesh,
        in_specs=placed,
        out_specs=(P("prompt", "slot", None, None), P("prompt", "slot")),
        check_vma=False,
    )
```

```python
import functools
import math

import jax
import jax.numpy as jnp
from jax import lax
from jax.experimental import pallas as pl
from jax.experimental.pallas import tpu as pltpu
from jax.sharding import PartitionSpec as P

HEADS = 64
KVH = 8
HD = 128
GROUPS = HEADS // KVH
SCALE = math.log2(math.e) / math.sqrt(HD)
LOW = -1e30
ROOM = 2.0**100
PARTS = ((0, 5), (5, 3))
LAST = 16
EMPTY = 1024.0
NT = (((1,), (1,)), ((), ()))


def lasting(microseconds):
    return pl.CostEstimate(flops=0, bytes_accessed=int(microseconds * 3.5e6), transcendentals=0)


PARAMS = pltpu.CompilerParams(vmem_limit_bytes=64 * 2**20)


def slot_of(judge, routes):
    tile, found = jnp.int32(0), jnp.bool_(False)
    for s in range(routes.shape[0]):
        here = routes[s] == judge
        tile, found = jnp.where(here, s, tile), found | here
    return tile, found


def pack_kernel(chips, parts, me, routes, mate_routes, *rest):
    tiles, outs = rest[: 2 * chips], list(rest[2 * chips :])
    chip, core = me[0] // 2, me[0] % 2
    top = (lax.broadcasted_iota(jnp.int32, (16, HD), 0) == 0) & (pl.program_id(0) == 0)
    for head_from, heads in parts:
        for offset in range(chips):
            out = outs.pop(0)
            for n, held in enumerate((routes, mate_routes)):
                tile = tiles[2 * offset + n]
                found = slot_of(2 * (chip ^ offset) + core, held)[1]
                for i in range(2 * heads):
                    first = (i % 2 * KVH + head_from + i // 2) * HD
                    out[n, :, i * HD : (i + 1) * HD] = tile[0, :, first : first + HD]
                mark = top & jnp.logical_not(found)
                kept = tile[0, :16, head_from * HD : (head_from + 1) * HD]
                out[n, :16, :HD] = jnp.where(mark, jnp.full_like(kept, EMPTY), kept)


def pack(parts, chips, me, routes, mate_routes, patch, mate_patch):
    tile_rows, width = patch.shape[1:]
    rows = tile_rows // 4
    shapes, specs, sources = [], [], []
    for _, heads in parts:
        shapes += [(2, tile_rows, 2 * heads * HD)] * chips
        specs += [pl.BlockSpec((2, rows, 2 * heads * HD), lambda r, *_: (0, r, 0))] * chips
    for offset in range(chips):
        for n in range(2):

            def source(r, me, *held, offset=offset, n=n):
                judge = 2 * ((me[0] // 2) ^ offset) + me[0] % 2
                return slot_of(judge, held[n])[0], r, 0

            sources.append(pl.BlockSpec((1, rows, width), source))
    return pl.pallas_call(
        functools.partial(pack_kernel, chips, parts),
        out_shape=[jax.ShapeDtypeStruct(shape, patch.dtype) for shape in shapes],
        grid_spec=pltpu.PrefetchScalarGridSpec(
            num_scalar_prefetch=3,
            grid=(tile_rows // rows,),
            in_specs=sources,
            out_specs=specs,
        ),
        compiler_params=PARAMS,
        cost_estimate=lasting(5),
        name="pack_tiles",
    )(me, routes, mate_routes, *([patch, mate_patch] * chips))


def pipelined(scores, finish):
    held = scores(0)
    for h in range(1, GROUPS):
        following = scores(h)
        finish(held, h - 1)
        held = following
    finish(held, GROUPS - 1)


def fill_text(me, length, head, blocks, sk_ref, sv_ref, held, kbuf, vbuf):
    prefix_rows, columns = blocks[0].shape
    live = lax.broadcasted_iota(jnp.int32, (prefix_rows, HD), 0) < length[0]

    @pl.when(pl.program_id(0) == 0)
    def _():
        chip, core = me[0] // 2, me[0] % 2
        for n, block in enumerate(blocks):
            held[2 * (chip ^ (n // 2)) + (core ^ (n % 2))] = block[...]
        vbuf[:prefix_rows, HD:] = live.astype(vbuf.dtype)
        vbuf[prefix_rows:, HD:] = jnp.ones((sk_ref.shape[0], HD), vbuf.dtype)

    for buf, column, ref in ((kbuf, head, sk_ref), (vbuf, KVH + head, sv_ref)):
        owner, within = column // (columns // HD), column % (columns // HD)
        rows = held[owner, :, pl.ds(pl.multiple_of(within * HD, HD), HD)]
        other = rows[0:1, :] if buf is kbuf else jnp.zeros_like(rows)
        buf[:prefix_rows, :HD] = jnp.where(live, rows, other)
        buf[prefix_rows:, :HD] = ref[...]


def text_kernel(slots, me, length, q_ref, *rest):
    blocks, (sk_ref, sv_ref, o_ref, stat_ref, kv_ref, held, kbuf, vbuf) = rest[:slots], rest[slots:]
    suffix_rows = sk_ref.shape[0]
    prefix_rows = kbuf.shape[0] - suffix_rows
    fill_text(me, length, pl.program_id(0), blocks, sk_ref, sv_ref, held, kbuf, vbuf)
    kv_ref[0, :, :HD] = kbuf[...]
    kv_ref[0, :, HD:] = vbuf[:, :HD]
    causal = lax.broadcasted_iota(jnp.int32, (suffix_rows, suffix_rows), 1) <= lax.broadcasted_iota(
        jnp.int32, (suffix_rows, suffix_rows), 0
    )

    lane = lax.broadcasted_iota(jnp.int32, (suffix_rows, HD), 1)

    def scores(h):
        s = lax.dot_general(
            q_ref[:, h * HD : (h + 1) * HD], kbuf[...], NT, preferred_element_type=jnp.float32
        )
        return jnp.concatenate(
            [s[:, :prefix_rows], jnp.where(causal, s[:, prefix_rows:], LOW)], axis=1
        )

    def finish(s, h):
        peak = jnp.max(s, axis=1, keepdims=True)
        weights = jnp.exp2((s - peak) * SCALE).astype(jnp.bfloat16)
        mixed = jnp.dot(weights, vbuf[...], preferred_element_type=jnp.float32)
        o_ref[:, h * HD : (h + 1) * HD] = mixed[:, :HD]
        held = jnp.where(lane == GROUPS + h, mixed[:, HD:], stat_ref[...])
        stat_ref[...] = jnp.where(lane == h, peak, held)

    pipelined(scores, finish)


def attend_text(me, length, queries, prefix, suffix):
    rows = queries.shape[0]
    total, wide = prefix[0].shape[0] + suffix.shape[0], GROUPS * HD
    column = lambda g, *_: (0, g)
    return pl.pallas_call(
        functools.partial(text_kernel, len(prefix)),
        out_shape=[
            jax.ShapeDtypeStruct(queries.shape, jnp.float32),
            jax.ShapeDtypeStruct((rows, KVH * HD), jnp.float32),
            jax.ShapeDtypeStruct((KVH, total, 2 * HD), queries.dtype),
        ],
        grid_spec=pltpu.PrefetchScalarGridSpec(
            num_scalar_prefetch=2,
            grid=(KVH,),
            in_specs=[pl.BlockSpec((rows, wide), column)]
            + [pl.BlockSpec(block.shape, lambda g, *_: (0, 0)) for block in prefix]
            + [
                pl.BlockSpec((suffix.shape[0], HD), column),
                pl.BlockSpec((suffix.shape[0], HD), lambda g, *_: (0, KVH + g)),
            ],
            out_specs=[
                pl.BlockSpec((rows, wide), column),
                pl.BlockSpec((rows, HD), column),
                pl.BlockSpec((1, total, 2 * HD), lambda g, *_: (g, 0, 0)),
            ],
            scratch_shapes=[
                pltpu.VMEM((len(prefix),) + prefix[0].shape, queries.dtype),
                pltpu.VMEM((total, HD), queries.dtype),
                pltpu.VMEM((total, 2 * HD), queries.dtype),
            ],
        ),
        compiler_params=PARAMS,
        cost_estimate=lasting(21),
        name="attend_text",
    )(me, length, queries, *prefix, suffix, suffix)


def tile_at(tiles, n):
    return tiles[n // 2].at[n % 2]


def place_tiles(slots, kept, tiles, place_ref):
    count = jnp.int32(0)
    for n in range(slots):
        found = jnp.max(tile_at(tiles, n)[0:1, :HD].astype(jnp.float32)) < EMPTY
        place_ref[n] = jnp.where(found, count, kept)
        count = count + jnp.where(found, 1, 0)


def fill_image(slots, head, tiles, place_ref, kbuf, vbuf):
    tile_rows = tiles[0].shape[-2]
    for n in range(slots):
        row = pl.ds(pl.multiple_of(place_ref[n] * tile_rows, tile_rows), tile_rows)
        tile = tile_at(tiles, n)
        for i, buf in enumerate((kbuf, vbuf)):
            first = (2 * head + i) * HD
            buf[row, :HD] = tile[:, first : first + HD]


def image_kernel(slots, kept, count, last, q_ref, acc_ref, stat_ref, *rest):
    tiles, rest = rest[:count], rest[count:]
    if last:
        length, last_ref, head_ref, text_ref, o_ref, score_ref, kbuf, vbuf, place_ref = rest[:9]
        kv_ref, sem = rest[9:]
        head_from, heads, prefix_rows = last
        copy = pltpu.make_async_copy(text_ref.at[pl.ds(head_from, heads)], kv_ref, sem)
    else:
        o_ref, kbuf, vbuf, place_ref = rest[-4:]
    tile_rows = tiles[0].shape[-2]
    total, rows = kept * tile_rows, q_ref.shape[0]
    g = pl.program_id(0)

    @pl.when(g == 0)
    def _():
        vbuf[:, :, HD:] = jnp.ones(vbuf.shape[:2] + (HD,), vbuf.dtype)
        place_tiles(slots, kept, tiles, place_ref)
        if last:
            copy.start()

    fill_image(slots, 0, tiles, place_ref, kbuf.at[g], vbuf.at[g])

    def scores(column):
        return lax.dot_general(
            q_ref[:, column], kbuf[g, :total], NT, preferred_element_type=jnp.float32
        )

    def close(summed, totals, column):
        o_ref[:, column] = (summed / totals).astype(o_ref.dtype)

    largest = [jnp.zeros((8, HD), jnp.float32)]

    def finish(s, h):
        column = slice(h * HD, (h + 1) * HD)
        held = stat_ref[:, h : h + 1]
        powers = []
        for k in range(total // HD):
            power = (s[:, k * HD : (k + 1) * HD] - held) * SCALE
            powers.append(jnp.exp2(power).astype(jnp.bfloat16))
        weights = jnp.concatenate(powers, axis=1)
        mixed = jnp.dot(weights, vbuf[g, :total], preferred_element_type=jnp.float32)
        totals = mixed[:, HD:] + stat_ref[:, GROUPS + h : GROUPS + h + 1]
        largest[0] = jnp.maximum(largest[0], jnp.max(totals.reshape(rows // 8, 8, HD), axis=0))
        close(mixed[:, :HD] + acc_ref[:, column], totals, column)

    pipelined(lambda h: scores(slice(h * HD, (h + 1) * HD)), finish)

    @pl.when(jnp.logical_not(jnp.max(largest[0]) < ROOM))
    def _():
        @pl.loop(0, GROUPS)
        def _(h):
            column = pl.ds(pl.multiple_of(h * HD, HD), HD)
            s = scores(column)
            lane = lax.broadcasted_iota(jnp.int32, (rows, HD), 1)
            held = jnp.sum(jnp.where(lane == h, stat_ref[...], 0.0), axis=1, keepdims=True)
            sums = jnp.where(lane == GROUPS + h, stat_ref[...], 0.0)
            sums = jnp.sum(sums, axis=1, keepdims=True)
            peak = jnp.maximum(held, jnp.max(s, axis=1, keepdims=True))
            weights = jnp.exp2((s - peak) * SCALE).astype(jnp.bfloat16)
            mixed = jnp.dot(weights, vbuf[g, :total], preferred_element_type=jnp.float32)
            fade = jnp.exp2((held - peak) * SCALE)
            summed = acc_ref[:, column] * fade + mixed[:, :HD]
            close(summed, sums * fade + mixed[:, HD:], column)

    if last:
        @pl.when(g == heads - 1)
        def _():
            copy.wait()
            score_ref[...] = last_row_gain(
                head_from, heads, prefix_rows, total, length, last_ref, head_ref, kv_ref, kbuf, vbuf
            )


def attend_image(chips, kept, part, tiles, queries, summed, stats, context=None, last=None):
    head_from, heads = part
    tile_rows = tiles[0].shape[-2]
    total, wide, rows = kept * tile_rows, GROUPS * HD, queries.shape[0]
    column = lambda g: (0, head_from + g)
    specs = [pl.BlockSpec((rows, wide), column)] * 2 + [pl.BlockSpec((rows, HD), column)]
    specs += [pl.BlockSpec((2, tile_rows, 2 * HD), lambda g: (0, 0, g)) for tile in tiles]
    operands = [queries, summed, stats, *tiles]
    shapes = [jax.ShapeDtypeStruct(queries.shape, queries.dtype)]
    outs = [pl.BlockSpec((rows, wide), column)]
    scratch = [
        pltpu.VMEM((heads, total + tile_rows, HD), queries.dtype),
        pltpu.VMEM((heads, total + tile_rows, 2 * HD), queries.dtype),
        pltpu.SMEM((2 * chips,), jnp.int32),
    ]
    aliases, static = {}, None
    if last is not None:
        length, prefix_rows, head, text_rows = last
        static = (head_from, heads, prefix_rows)
        end = rows // LAST - 1
        operands += [length, queries, head, text_rows]
        specs += [
            pl.BlockSpec(memory_space=pltpu.SMEM),
            pl.BlockSpec((LAST, queries.shape[1]), lambda g: (end, 0)),
            pl.BlockSpec(head.shape, lambda g: (0, 0)),
            pl.BlockSpec(memory_space=pl.ANY),
        ]
        shapes.append(jax.ShapeDtypeStruct((GROUPS, HD), jnp.float32))
        outs.append(pl.BlockSpec((GROUPS, HD), lambda g: (0, 0)))
        scratch += [
            pltpu.VMEM((heads,) + text_rows.shape[1:], queries.dtype),
            pltpu.SemaphoreType.DMA,
        ]
    if context is not None:
        aliases = {len(operands): 0}
        operands.append(context)
        specs.append(pl.BlockSpec(memory_space=pl.ANY))
    return pl.pallas_call(
        functools.partial(image_kernel, 2 * chips, kept, len(tiles), static),
        out_shape=shapes,
        grid=(heads,),
        in_specs=specs,
        out_specs=outs,
        scratch_shapes=scratch,
        input_output_aliases=aliases,
        compiler_params=PARAMS,
        cost_estimate=lasting(2 * heads),
        name="attend_image",
    )(*operands)


def last_row_gain(
    head_from, heads, prefix_rows, total, length, q_ref, head_ref, kv_ref, kbuf, vbuf
):
    gain = jnp.zeros((GROUPS, HD), jnp.float32)
    column = lax.broadcasted_iota(jnp.int32, (GROUPS, kv_ref.shape[1]), 1)
    live = (column < length[0]) | (column >= prefix_rows)
    for i in range(heads):
        first = (head_from + i) * GROUPS
        q = [q_ref[:, (first + h) * HD : (first + h + 1) * HD] for h in range(GROUPS)]
        q = jnp.concatenate([part.astype(jnp.float32)[-1:] for part in q], axis=0)
        q = q.astype(jnp.bfloat16)
        s = [
            lax.dot_general(q, keys, NT, preferred_element_type=jnp.float32)
            for keys in (kv_ref[i, :, :HD], kbuf[i, :total])
        ]
        s[0] = jnp.where(live, s[0], LOW)
        peak = jnp.maximum(*[jnp.max(part, axis=1, keepdims=True) for part in s])
        weights = [jnp.exp2((part - peak) * SCALE) for part in s]
        mixed = sum(
            jnp.dot(part.astype(jnp.bfloat16), values, preferred_element_type=jnp.float32)
            for part, values in zip(weights, (kv_ref[i, :, HD:], vbuf[i, :total, :HD]))
        )
        totals = sum(jnp.sum(part, axis=1, keepdims=True) for part in weights)
        out = (mixed / totals).astype(jnp.bfloat16).astype(jnp.float32)
        gain = gain + out * head_ref[first : first + GROUPS, :]
    return gain


def last_kernel(slots, kept, count, head_from, heads, prefix_rows, length, q_ref, head_ref, kv_ref, *rest):
    tiles, (before, score_ref, kbuf, vbuf, place_ref) = rest[:count], rest[count:]
    total = kept * tiles[0].shape[-2]
    place_tiles(slots, kept, tiles, place_ref)
    for i in range(heads):
        fill_image(slots, i, tiles, place_ref, kbuf.at[i], vbuf.at[i])
    gain = before[...] + last_row_gain(
        head_from, heads, prefix_rows, total, length, q_ref, head_ref, kv_ref, kbuf, vbuf
    )
    score_ref[...] = jnp.broadcast_to(jnp.sum(gain, axis=0, keepdims=True), score_ref.shape)


def last_scratch(heads, rows, dtype):
    return [pltpu.VMEM((heads, rows, HD), dtype)] * 2


def last_rows(chips, kept, part, tiles, queries, length, prefix_rows, head, text_rows, share, devices):
    head_from, heads = part
    tile_rows, text = tiles[0].shape[-2], text_rows.shape[1]
    whole = lambda x: pl.BlockSpec(x.shape, lambda g, d=x.ndim: (0,) * d)
    end = queries.shape[0] // LAST - 1
    specs = [
        pl.BlockSpec(memory_space=pltpu.SMEM),
        pl.BlockSpec((LAST, queries.shape[1]), lambda g: (end, 0)),
        whole(head),
        pl.BlockSpec(
            (pl.Element(heads), pl.Element(text), pl.Element(2 * HD)), lambda g: (head_from, 0, 0)
        ),
    ]
    shape = (devices, HD)
    return pl.pallas_call(
        functools.partial(
            last_kernel, 2 * chips, kept, len(tiles), head_from, heads, prefix_rows
        ),
        out_shape=jax.ShapeDtypeStruct(shape, jnp.float32),
        grid=(1,),
        in_specs=specs + [whole(tile) for tile in tiles] + [whole(share)],
        out_specs=pl.BlockSpec(shape, lambda g: (0, 0)),
        scratch_shapes=last_scratch(heads, (kept + 1) * tile_rows, queries.dtype)
        + [pltpu.SMEM((2 * chips,), jnp.int32)],
        compiler_params=PARAMS,
        cost_estimate=lasting(heads),
        name="last_rows",
    )(length, queries, head, text_rows, *tiles, share)


def normalize_kernel(prompts, slots, every_ref, out_ref):
    own = lax.axis_index("prompt") * slots + lax.axis_index("slot")
    score = jnp.sum(every_ref[...], axis=1, keepdims=True)
    score = jnp.broadcast_to(score, every_ref.shape).reshape(prompts, slots, HD)
    deviation = score - jnp.sum(score, axis=1, keepdims=True) / slots
    spread = jnp.sum(jnp.sum(deviation * deviation, axis=0), axis=0, keepdims=True)
    advantage = deviation / jnp.sqrt(spread / (prompts * slots) + 1e-06)
    advantage = advantage.reshape(prompts * slots, HD)
    row = lax.broadcasted_iota(jnp.int32, advantage.shape, 0)
    out_ref[...] = jnp.sum(jnp.where(row == own, advantage, 0.0), axis=0, keepdims=True)[:, :1]


def per_device(patch_kv, routes, prefix_kv, prefix_len, queries, suffix_kv, score_head):
    slot_count = lax.axis_size("slot")
    prompt_count = lax.axis_size("prompt")
    chips = slot_count // 2
    kept = slot_count // 2
    me = lax.axis_index("slot").astype(jnp.int32).reshape(1)

    def swap(x, k):
        return lax.ppermute(x, "slot", [(i, i ^ k) for i in range(slot_count)])

    mate_patch, mate_routes = swap(patch_kv[0], 1), swap(routes[0], 1)
    near = [prefix_kv[0]] + [swap(prefix_kv[0], 2 * offset) for offset in range(1, chips)]
    buffers = pack(PARTS, chips, me, routes[0], mate_routes, patch_kv[0], mate_patch)
    held = lax.optimization_barrier((near[1:], buffers[0]))[0]
    far = [swap(block, 1) for block in [near[0], *held]]
    first, second = list(buffers[:chips]), list(buffers[chips:])
    for n in range(1, chips):
        first[n] = lax.optimization_barrier((first[n], near[:-1] if n == chips - 1 else near))[0]
    prefix = [block for pair in zip(near, far) for block in pair]
    suffix = suffix_kv[0, 0]
    summed, stats, text_rows = attend_text(me, prefix_len, queries[0, 0], prefix, suffix)

    second[-1] = lax.optimization_barrier((second[-1], stats))[0]
    arrived = [
        [sent[0]] + [swap(sent[offset], 2 * offset) for offset in range(1, chips)]
        for sent in (first, second)
    ]
    head = score_head.reshape(HEADS, HD)
    last = (prefix_len, prefix_kv.shape[1], head, text_rows)
    main = (queries[0, 0], summed, stats)
    context, share = attend_image(chips, kept, PARTS[0], arrived[0], *main, last=last)
    devices = prompt_count * slot_count
    shares = last_rows(chips, kept, PARTS[1], arrived[1], queries[0, 0], *last, share, devices)
    every = lax.all_to_all(shares, ("prompt", "slot"), 0, 0, tiled=True)
    (context,) = attend_image(chips, kept, PARTS[1], arrived[1], *main, context)
    advantage = pl.pallas_call(
        functools.partial(normalize_kernel, prompt_count, slot_count),
        out_shape=jax.ShapeDtypeStruct((1, 1), jnp.float32),
        in_specs=[pl.BlockSpec(memory_space=pltpu.VMEM)],
        out_specs=pl.BlockSpec(memory_space=pltpu.VMEM),
        cost_estimate=lasting(1),
        name="normalize",
    )(every)
    return (context[None, None], advantage)


def solution(mesh):
    placed = (
        P("prompt", "slot", None, None),
        P("prompt", "slot"),
        P("prompt", None, "slot"),
        P("prompt"),
        P("prompt", "slot", None, None),
        P("prompt", "slot", None, None),
        P(),
    )
    return jax.shard_map(
        per_device,
        mesh=mesh,
        in_specs=placed,
        out_specs=(P("prompt", "slot", None, None), P("prompt", "slot")),
        check_vma=False,
    )
```

```python
import functools
import math

import jax
import jax.numpy as jnp
from jax import lax
from jax.experimental import pallas as pl
from jax.experimental.pallas import tpu as pltpu
from jax.sharding import PartitionSpec as P

HEADS = 64
KVH = 8
HD = 128
GROUPS = HEADS // KVH
SCALE = math.log2(math.e) / math.sqrt(HD)
LOW = -1e30
ROOM = 2.0**100
PARTS = ((0, 5), (5, 3))
LAST = 16
EMPTY = 1024.0
NT = (((1,), (1,)), ((), ()))


def lasting(microseconds):
    return pl.CostEstimate(flops=0, bytes_accessed=int(microseconds * 3.5e6), transcendentals=0)


PARAMS = pltpu.CompilerParams(vmem_limit_bytes=64 * 2**20)


def pack_kernel(chips, parts, held, mate_held, *rest):
    tiles, outs = rest[: 2 * chips], list(rest[2 * chips :])
    top = (lax.broadcasted_iota(jnp.int32, (16, HD), 0) == 0) & (pl.program_id(0) == 0)
    for head_from, heads in parts:
        for offset in range(chips):
            out = outs.pop(0)
            for n, table in enumerate((held, mate_held)):
                tile = tiles[2 * offset + n]
                for i in range(2 * heads):
                    first = (i % 2 * KVH + head_from + i // 2) * HD
                    out[n, :, i * HD : (i + 1) * HD] = tile[0, :, first : first + HD]
                mark = top & (table[offset] < 0)
                kept = tile[0, :16, head_from * HD : (head_from + 1) * HD]
                out[n, :16, :HD] = jnp.where(mark, jnp.full_like(kept, EMPTY), kept)


def pack(parts, chips, held, mate_held, patch, mate_patch):
    tile_rows, width = patch.shape[1:]
    rows = tile_rows // 2
    shapes, specs, sources = [], [], []
    for _, heads in parts:
        shapes += [(2, tile_rows, 2 * heads * HD)] * chips
        specs += [pl.BlockSpec((2, rows, 2 * heads * HD), lambda r, *_: (0, r, 0))] * chips
    for offset in range(chips):
        for n in range(2):

            def source(r, *tables, offset=offset, n=n):
                return jnp.maximum(tables[n][offset], 0), r, 0

            sources.append(pl.BlockSpec((1, rows, width), source))
    return pl.pallas_call(
        functools.partial(pack_kernel, chips, parts),
        out_shape=[jax.ShapeDtypeStruct(shape, patch.dtype) for shape in shapes],
        grid_spec=pltpu.PrefetchScalarGridSpec(
            num_scalar_prefetch=2,
            grid=(tile_rows // rows,),
            in_specs=sources,
            out_specs=specs,
        ),
        compiler_params=PARAMS,
        cost_estimate=lasting(5),
        name="pack_tiles",
    )(held, mate_held, *([patch, mate_patch] * chips))


def pipelined(scores, finish):
    held = scores(0)
    for h in range(1, GROUPS):
        following = scores(h)
        finish(held, h - 1)
        held = following
    finish(held, GROUPS - 1)


def fill_text(me, length, head, blocks, sk_ref, sv_ref, held, kbuf, vbuf):
    prefix_rows, columns = blocks[0].shape
    live = lax.broadcasted_iota(jnp.int32, (prefix_rows, HD), 0) < length[0]

    @pl.when(pl.program_id(0) == 0)
    def _():
        chip, core = me[0] // 2, me[0] % 2
        for n, block in enumerate(blocks):
            held[2 * (chip ^ (n // 2)) + (core ^ (n % 2))] = block[...]
        vbuf[:prefix_rows, HD:] = live.astype(vbuf.dtype)
        vbuf[prefix_rows:, HD:] = jnp.ones((sk_ref.shape[0], HD), vbuf.dtype)

    for buf, column, ref in ((kbuf, head, sk_ref), (vbuf, KVH + head, sv_ref)):
        owner, within = column // (columns // HD), column % (columns // HD)
        rows = held[owner, :, pl.ds(pl.multiple_of(within * HD, HD), HD)]
        other = rows[0:1, :] if buf is kbuf else jnp.zeros_like(rows)
        buf[:prefix_rows, :HD] = jnp.where(live, rows, other)
        buf[prefix_rows:, :HD] = ref[...]


def text_kernel(slots, me, length, q_ref, *rest):
    blocks, (sk_ref, sv_ref, o_ref, stat_ref, kv_ref, held, kbuf, vbuf) = rest[:slots], rest[slots:]
    suffix_rows = sk_ref.shape[0]
    prefix_rows = kbuf.shape[0] - suffix_rows
    fill_text(me, length, pl.program_id(0), blocks, sk_ref, sv_ref, held, kbuf, vbuf)
    kv_ref[0, :, :HD] = kbuf[...]
    kv_ref[0, :, HD:] = vbuf[:, :HD]
    causal = lax.broadcasted_iota(jnp.int32, (suffix_rows, suffix_rows), 1) <= lax.broadcasted_iota(
        jnp.int32, (suffix_rows, suffix_rows), 0
    )

    lane = lax.broadcasted_iota(jnp.int32, (suffix_rows, HD), 1)

    def scores(h):
        s = lax.dot_general(
            q_ref[:, h * HD : (h + 1) * HD], kbuf[...], NT, preferred_element_type=jnp.float32
        )
        return jnp.concatenate(
            [s[:, :prefix_rows], jnp.where(causal, s[:, prefix_rows:], LOW)], axis=1
        )

    def finish(s, h):
        peak = jnp.max(s, axis=1, keepdims=True)
        weights = jnp.exp2((s - peak) * SCALE).astype(jnp.bfloat16)
        mixed = jnp.dot(weights, vbuf[...], preferred_element_type=jnp.float32)
        o_ref[:, h * HD : (h + 1) * HD] = mixed[:, :HD]
        held = jnp.where(lane == GROUPS + h, mixed[:, HD:], stat_ref[...])
        stat_ref[...] = jnp.where(lane == h, peak, held)

    pipelined(scores, finish)


def attend_text(me, length, queries, prefix, suffix):
    rows = queries.shape[0]
    total, wide = prefix[0].shape[0] + suffix.shape[0], GROUPS * HD
    column = lambda g, *_: (0, g)
    return pl.pallas_call(
        functools.partial(text_kernel, len(prefix)),
        out_shape=[
            jax.ShapeDtypeStruct(queries.shape, jnp.float32),
            jax.ShapeDtypeStruct((rows, KVH * HD), jnp.float32),
            jax.ShapeDtypeStruct((KVH, total, 2 * HD), queries.dtype),
        ],
        grid_spec=pltpu.PrefetchScalarGridSpec(
            num_scalar_prefetch=2,
            grid=(KVH,),
            in_specs=[pl.BlockSpec((rows, wide), column)]
            + [pl.BlockSpec(block.shape, lambda g, *_: (0, 0)) for block in prefix]
            + [
                pl.BlockSpec((suffix.shape[0], HD), column),
                pl.BlockSpec((suffix.shape[0], HD), lambda g, *_: (0, KVH + g)),
            ],
            out_specs=[
                pl.BlockSpec((rows, wide), column),
                pl.BlockSpec((rows, HD), column),
                pl.BlockSpec((1, total, 2 * HD), lambda g, *_: (g, 0, 0)),
            ],
            scratch_shapes=[
                pltpu.VMEM((len(prefix),) + prefix[0].shape, queries.dtype),
                pltpu.VMEM((total, HD), queries.dtype),
                pltpu.VMEM((total, 2 * HD), queries.dtype),
            ],
        ),
        compiler_params=PARAMS,
        cost_estimate=lasting(21),
        name="attend_text",
    )(me, length, queries, *prefix, suffix, suffix)


def tile_at(tiles, n):
    return tiles[n // 2].at[n % 2]


def place_tiles(slots, kept, tiles, place_ref):
    count = jnp.int32(0)
    for n in range(slots):
        found = jnp.max(tile_at(tiles, n)[0:1, :HD].astype(jnp.float32)) < EMPTY
        place_ref[n] = jnp.where(found, count, kept)
        count = count + jnp.where(found, 1, 0)


def fill_image(slots, head, tiles, place_ref, kbuf, vbuf):
    tile_rows = tiles[0].shape[-2]
    for n in range(slots):
        row = pl.ds(pl.multiple_of(place_ref[n] * tile_rows, tile_rows), tile_rows)
        tile = tile_at(tiles, n)
        for i, buf in enumerate((kbuf, vbuf)):
            first = (2 * head + i) * HD
            buf[row, :HD] = tile[:, first : first + HD]


def image_kernel(slots, kept, count, last, q_ref, acc_ref, stat_ref, *rest):
    tiles, rest = rest[:count], rest[count:]
    if last:
        length, last_ref, head_ref, text_ref, o_ref, score_ref, kbuf, vbuf, place_ref = rest[:9]
        kv_ref, sem = rest[9:]
        head_from, heads, prefix_rows = last
        copy = pltpu.make_async_copy(text_ref.at[pl.ds(head_from, heads)], kv_ref, sem)
    else:
        o_ref, kbuf, vbuf, place_ref = rest[-4:]
    tile_rows = tiles[0].shape[-2]
    total, rows = kept * tile_rows, q_ref.shape[0]
    g = pl.program_id(0)

    @pl.when(g == 0)
    def _():
        vbuf[:, :, HD:] = jnp.ones(vbuf.shape[:2] + (HD,), vbuf.dtype)
        place_tiles(slots, kept, tiles, place_ref)
        if last:
            copy.start()

    fill_image(slots, 0, tiles, place_ref, kbuf.at[g], vbuf.at[g])

    def scores(column):
        return lax.dot_general(
            q_ref[:, column], kbuf[g, :total], NT, preferred_element_type=jnp.float32
        )

    def close(summed, totals, column):
        o_ref[:, column] = (summed / totals).astype(o_ref.dtype)

    largest = [jnp.zeros((8, HD), jnp.float32)]

    def finish(s, h):
        column = slice(h * HD, (h + 1) * HD)
        held = stat_ref[:, h : h + 1]
        powers = []
        for k in range(total // HD):
            power = (s[:, k * HD : (k + 1) * HD] - held) * SCALE
            powers.append(jnp.exp2(power).astype(jnp.bfloat16))
        weights = jnp.concatenate(powers, axis=1)
        mixed = jnp.dot(weights, vbuf[g, :total], preferred_element_type=jnp.float32)
        totals = mixed[:, HD:] + stat_ref[:, GROUPS + h : GROUPS + h + 1]
        largest[0] = jnp.maximum(largest[0], jnp.max(totals.reshape(rows // 8, 8, HD), axis=0))
        close(mixed[:, :HD] + acc_ref[:, column], totals, column)

    pipelined(lambda h: scores(slice(h * HD, (h + 1) * HD)), finish)

    @pl.when(jnp.logical_not(jnp.max(largest[0]) < ROOM))
    def _():
        @pl.loop(0, GROUPS)
        def _(h):
            column = pl.ds(pl.multiple_of(h * HD, HD), HD)
            s = scores(column)
            lane = lax.broadcasted_iota(jnp.int32, (rows, HD), 1)
            held = jnp.sum(jnp.where(lane == h, stat_ref[...], 0.0), axis=1, keepdims=True)
            sums = jnp.where(lane == GROUPS + h, stat_ref[...], 0.0)
            sums = jnp.sum(sums, axis=1, keepdims=True)
            peak = jnp.maximum(held, jnp.max(s, axis=1, keepdims=True))
            weights = jnp.exp2((s - peak) * SCALE).astype(jnp.bfloat16)
            mixed = jnp.dot(weights, vbuf[g, :total], preferred_element_type=jnp.float32)
            fade = jnp.exp2((held - peak) * SCALE)
            summed = acc_ref[:, column] * fade + mixed[:, :HD]
            close(summed, sums * fade + mixed[:, HD:], column)

    if last:
        @pl.when(g == heads - 1)
        def _():
            copy.wait()
            score_ref[...] = last_row_gain(
                head_from, heads, prefix_rows, total, length, last_ref, head_ref, kv_ref, kbuf, vbuf
            )


def attend_image(chips, kept, part, tiles, queries, summed, stats, context=None, last=None):
    head_from, heads = part
    tile_rows = tiles[0].shape[-2]
    total, wide, rows = kept * tile_rows, GROUPS * HD, queries.shape[0]
    column = lambda g: (0, head_from + g)
    specs = [pl.BlockSpec((rows, wide), column)] * 2 + [pl.BlockSpec((rows, HD), column)]
    specs += [pl.BlockSpec((2, tile_rows, 2 * HD), lambda g: (0, 0, g)) for tile in tiles]
    operands = [queries, summed, stats, *tiles]
    shapes = [jax.ShapeDtypeStruct(queries.shape, queries.dtype)]
    outs = [pl.BlockSpec((rows, wide), column)]
    scratch = [
        pltpu.VMEM((heads, total + tile_rows, HD), queries.dtype),
        pltpu.VMEM((heads, total + tile_rows, 2 * HD), queries.dtype),
        pltpu.SMEM((2 * chips,), jnp.int32),
    ]
    aliases, static = {}, None
    if last is not None:
        length, prefix_rows, head, text_rows = last
        static = (head_from, heads, prefix_rows)
        end = rows // LAST - 1
        operands += [length, queries, head, text_rows]
        specs += [
            pl.BlockSpec(memory_space=pltpu.SMEM),
            pl.BlockSpec((LAST, queries.shape[1]), lambda g: (end, 0)),
            pl.BlockSpec(head.shape, lambda g: (0, 0)),
            pl.BlockSpec(memory_space=pl.ANY),
        ]
        shapes.append(jax.ShapeDtypeStruct((GROUPS, HD), jnp.float32))
        outs.append(pl.BlockSpec((GROUPS, HD), lambda g: (0, 0)))
        scratch += [
            pltpu.VMEM((heads,) + text_rows.shape[1:], queries.dtype),
            pltpu.SemaphoreType.DMA,
        ]
    if context is not None:
        aliases = {len(operands): 0}
        operands.append(context)
        specs.append(pl.BlockSpec(memory_space=pl.ANY))
    return pl.pallas_call(
        functools.partial(image_kernel, 2 * chips, kept, len(tiles), static),
        out_shape=shapes,
        grid=(heads,),
        in_specs=specs,
        out_specs=outs,
        scratch_shapes=scratch,
        input_output_aliases=aliases,
        compiler_params=PARAMS,
        cost_estimate=lasting(2 * heads),
        name="attend_image",
    )(*operands)


def last_row_gain(
    head_from, heads, prefix_rows, total, length, q_ref, head_ref, kv_ref, kbuf, vbuf
):
    gain = jnp.zeros((GROUPS, HD), jnp.float32)
    column = lax.broadcasted_iota(jnp.int32, (GROUPS, kv_ref.shape[1]), 1)
    live = (column < length[0]) | (column >= prefix_rows)
    for i in range(heads):
        first = (head_from + i) * GROUPS
        q = [q_ref[:, (first + h) * HD : (first + h + 1) * HD] for h in range(GROUPS)]
        q = jnp.concatenate([part.astype(jnp.float32)[-1:] for part in q], axis=0)
        q = q.astype(jnp.bfloat16)
        s = [
            lax.dot_general(q, keys, NT, preferred_element_type=jnp.float32)
            for keys in (kv_ref[i, :, :HD], kbuf[i, :total])
        ]
        s[0] = jnp.where(live, s[0], LOW)
        peak = jnp.maximum(*[jnp.max(part, axis=1, keepdims=True) for part in s])
        weights = [jnp.exp2((part - peak) * SCALE) for part in s]
        mixed = sum(
            jnp.dot(part.astype(jnp.bfloat16), values, preferred_element_type=jnp.float32)
            for part, values in zip(weights, (kv_ref[i, :, HD:], vbuf[i, :total, :HD]))
        )
        totals = sum(jnp.sum(part, axis=1, keepdims=True) for part in weights)
        out = (mixed / totals).astype(jnp.bfloat16).astype(jnp.float32)
        gain = gain + out * head_ref[first : first + GROUPS, :]
    return gain


def last_kernel(slots, kept, count, head_from, heads, prefix_rows, length, q_ref, head_ref, kv_ref, *rest):
    tiles, (before, score_ref, kbuf, vbuf, place_ref) = rest[:count], rest[count:]
    total = kept * tiles[0].shape[-2]
    place_tiles(slots, kept, tiles, place_ref)
    for i in range(heads):
        fill_image(slots, i, tiles, place_ref, kbuf.at[i], vbuf.at[i])
    gain = before[...] + last_row_gain(
        head_from, heads, prefix_rows, total, length, q_ref, head_ref, kv_ref, kbuf, vbuf
    )
    score_ref[...] = jnp.broadcast_to(jnp.sum(gain, axis=0, keepdims=True), score_ref.shape)


def last_scratch(heads, rows, dtype):
    return [pltpu.VMEM((heads, rows, HD), dtype)] * 2


def last_rows(chips, kept, part, tiles, queries, length, prefix_rows, head, text_rows, share, devices):
    head_from, heads = part
    tile_rows, text = tiles[0].shape[-2], text_rows.shape[1]
    whole = lambda x: pl.BlockSpec(x.shape, lambda g, d=x.ndim: (0,) * d)
    end = queries.shape[0] // LAST - 1
    specs = [
        pl.BlockSpec(memory_space=pltpu.SMEM),
        pl.BlockSpec((LAST, queries.shape[1]), lambda g: (end, 0)),
        whole(head),
        pl.BlockSpec(
            (pl.Element(heads), pl.Element(text), pl.Element(2 * HD)), lambda g: (head_from, 0, 0)
        ),
    ]
    shape = (devices, HD)
    return pl.pallas_call(
        functools.partial(
            last_kernel, 2 * chips, kept, len(tiles), head_from, heads, prefix_rows
        ),
        out_shape=jax.ShapeDtypeStruct(shape, jnp.float32),
        grid=(1,),
        in_specs=specs + [whole(tile) for tile in tiles] + [whole(share)],
        out_specs=pl.BlockSpec(shape, lambda g: (0, 0)),
        scratch_shapes=last_scratch(heads, (kept + 1) * tile_rows, queries.dtype)
        + [pltpu.SMEM((2 * chips,), jnp.int32)],
        compiler_params=PARAMS,
        cost_estimate=lasting(heads),
        name="last_rows",
    )(length, queries, head, text_rows, *tiles, share)


def normalize_kernel(prompts, slots, every_ref, out_ref):
    own = lax.axis_index("prompt") * slots + lax.axis_index("slot")
    score = jnp.sum(every_ref[...], axis=1, keepdims=True)
    score = jnp.broadcast_to(score, every_ref.shape).reshape(prompts, slots, HD)
    deviation = score - jnp.sum(score, axis=1, keepdims=True) / slots
    spread = jnp.sum(jnp.sum(deviation * deviation, axis=0), axis=0, keepdims=True)
    advantage = deviation / jnp.sqrt(spread / (prompts * slots) + 1e-06)
    advantage = advantage.reshape(prompts * slots, HD)
    row = lax.broadcasted_iota(jnp.int32, advantage.shape, 0)
    out_ref[...] = jnp.sum(jnp.where(row == own, advantage, 0.0), axis=0, keepdims=True)[:, :1]


def per_device(patch_kv, routes, prefix_kv, prefix_len, queries, suffix_kv, score_head):
    slot_count = lax.axis_size("slot")
    prompt_count = lax.axis_size("prompt")
    chips = slot_count // 2
    kept = slot_count // 2
    me = lax.axis_index("slot").astype(jnp.int32).reshape(1)

    def swap(x, k):
        return lax.ppermute(x, "slot", [(i, i ^ k) for i in range(slot_count)])

    slot = jnp.arange(routes.shape[1], dtype=jnp.int32)
    judges = 2 * (jnp.arange(chips, dtype=jnp.int32) ^ (me // 2)) + me % 2
    held, for_mate = [
        jnp.max(jnp.where(routes == judge[:, None], slot, -1), axis=1)
        for judge in (judges, judges ^ 1)
    ]
    mate_patch, mate_held = swap(patch_kv[0], 1), swap(for_mate, 1)
    near = [prefix_kv[0]] + [swap(prefix_kv[0], 2 * offset) for offset in range(1, chips)]
    buffers = pack(PARTS, chips, held, mate_held, patch_kv[0], mate_patch)
    come = lax.optimization_barrier((near[1:], buffers[0]))[0]
    far = [swap(block, 1) for block in [near[0], *come]]
    first, second = list(buffers[:chips]), list(buffers[chips:])
    for n in range(1, chips):
        first[n] = lax.optimization_barrier((first[n], near[:-1] if n == chips - 1 else near))[0]
    prefix = [block for pair in zip(near, far) for block in pair]
    suffix = suffix_kv[0, 0]
    summed, stats, text_rows = attend_text(me, prefix_len, queries[0, 0], prefix, suffix)

    second[-1] = lax.optimization_barrier((second[-1], stats))[0]
    arrived = [
        [sent[0]] + [swap(sent[offset], 2 * offset) for offset in range(1, chips)]
        for sent in (first, second)
    ]
    head = score_head.reshape(HEADS, HD)
    last = (prefix_len, prefix_kv.shape[1], head, text_rows)
    main = (queries[0, 0], summed, stats)
    context, share = attend_image(chips, kept, PARTS[0], arrived[0], *main, last=last)
    devices = prompt_count * slot_count
    shares = last_rows(chips, kept, PARTS[1], arrived[1], queries[0, 0], *last, share, devices)
    every = lax.all_to_all(shares, ("prompt", "slot"), 0, 0, tiled=True)
    (context,) = attend_image(chips, kept, PARTS[1], arrived[1], *main, context)
    advantage = pl.pallas_call(
        functools.partial(normalize_kernel, prompt_count, slot_count),
        out_shape=jax.ShapeDtypeStruct((1, 1), jnp.float32),
        in_specs=[pl.BlockSpec(memory_space=pltpu.VMEM)],
        out_specs=pl.BlockSpec(memory_space=pltpu.VMEM),
        cost_estimate=lasting(1),
        name="normalize",
    )(every)
    return (context[None, None], advantage)


def solution(mesh):
    placed = (
        P("prompt", "slot", None, None),
        P("prompt", "slot"),
        P("prompt", None, "slot"),
        P("prompt"),
        P("prompt", "slot", None, None),
        P("prompt", "slot", None, None),
        P(),
    )
    return jax.shard_map(
        per_device,
        mesh=mesh,
        in_specs=placed,
        out_specs=(P("prompt", "slot", None, None), P("prompt", "slot")),
        check_vma=False,
    )
```

```python
import functools
import math

import jax
import jax.numpy as jnp
from jax import lax
from jax.experimental import pallas as pl
from jax.experimental.pallas import tpu as pltpu
from jax.sharding import PartitionSpec as P

HEADS = 64
KVH = 8
HD = 128
GROUPS = HEADS // KVH
SCALE = math.log2(math.e) / math.sqrt(HD)
LOW = -1e30
ROOM = 2.0**100
PARTS = ((0, 5), (5, 3))
LAST = 16
EMPTY = 1024.0
NT = (((1,), (1,)), ((), ()))


def lasting(microseconds):
    return pl.CostEstimate(flops=0, bytes_accessed=int(microseconds * 3.5e6), transcendentals=0)


PARAMS = pltpu.CompilerParams(vmem_limit_bytes=64 * 2**20)


def pack_kernel(chips, parts, held, mate_held, *rest):
    tiles, outs = rest[: 2 * chips], list(rest[2 * chips :])
    top = (lax.broadcasted_iota(jnp.int32, (16, HD), 0) == 0) & (pl.program_id(0) == 0)
    for head_from, heads in parts:
        for offset in range(chips):
            out = outs.pop(0)
            for n, table in enumerate((held, mate_held)):
                tile = tiles[2 * offset + n]
                for i in range(2 * heads):
                    first = (i % 2 * KVH + head_from + i // 2) * HD
                    out[n, :, i * HD : (i + 1) * HD] = tile[0, :, first : first + HD]
                mark = top & (table[offset] < 0)
                kept = tile[0, :16, head_from * HD : (head_from + 1) * HD]
                out[n, :16, :HD] = jnp.where(mark, jnp.full_like(kept, EMPTY), kept)


def pack(parts, chips, held, mate_held, patch, mate_patch):
    tile_rows, width = patch.shape[1:]
    rows = tile_rows // 2
    shapes, specs, sources = [], [], []
    for _, heads in parts:
        shapes += [(2, tile_rows, 2 * heads * HD)] * chips
        specs += [pl.BlockSpec((2, rows, 2 * heads * HD), lambda r, *_: (0, r, 0))] * chips
    for offset in range(chips):
        for n in range(2):

            def source(r, *tables, offset=offset, n=n):
                return jnp.maximum(tables[n][offset], 0), r, 0

            sources.append(pl.BlockSpec((1, rows, width), source))
    return pl.pallas_call(
        functools.partial(pack_kernel, chips, parts),
        out_shape=[jax.ShapeDtypeStruct(shape, patch.dtype) for shape in shapes],
        grid_spec=pltpu.PrefetchScalarGridSpec(
            num_scalar_prefetch=2,
            grid=(tile_rows // rows,),
            in_specs=sources,
            out_specs=specs,
        ),
        compiler_params=PARAMS,
        cost_estimate=lasting(5),
        name="pack_tiles",
    )(held, mate_held, *([patch, mate_patch] * chips))


def pipelined(scores, finish):
    held = [scores(0), scores(1)]
    for h in range(GROUPS):
        if h + 2 < GROUPS:
            held.append(scores(h + 2))
        finish(held.pop(0), h)


def fill_text(me, length, head, blocks, sk_ref, sv_ref, held, kbuf, vbuf):
    prefix_rows, columns = blocks[0].shape
    live = lax.broadcasted_iota(jnp.int32, (prefix_rows, HD), 0) < length[0]

    @pl.when(pl.program_id(0) == 0)
    def _():
        chip, core = me[0] // 2, me[0] % 2
        for n, block in enumerate(blocks):
            held[2 * (chip ^ (n // 2)) + (core ^ (n % 2))] = block[...]
        vbuf[:prefix_rows, HD:] = live.astype(vbuf.dtype)
        vbuf[prefix_rows:, HD:] = jnp.ones((sk_ref.shape[0], HD), vbuf.dtype)

    for buf, column, ref in ((kbuf, head, sk_ref), (vbuf, KVH + head, sv_ref)):
        owner, within = column // (columns // HD), column % (columns // HD)
        rows = held[owner, :, pl.ds(pl.multiple_of(within * HD, HD), HD)]
        other = rows[0:1, :] if buf is kbuf else jnp.zeros_like(rows)
        buf[:prefix_rows, :HD] = jnp.where(live, rows, other)
        buf[prefix_rows:, :HD] = ref[...]


def text_kernel(slots, me, length, q_ref, *rest):
    blocks, (sk_ref, sv_ref, o_ref, stat_ref, kv_ref, held, kbuf, vbuf) = rest[:slots], rest[slots:]
    suffix_rows = sk_ref.shape[0]
    prefix_rows = kbuf.shape[0] - suffix_rows
    fill_text(me, length, pl.program_id(0), blocks, sk_ref, sv_ref, held, kbuf, vbuf)
    kv_ref[0, :, :HD] = kbuf[...]
    kv_ref[0, :, HD:] = vbuf[:, :HD]
    causal = lax.broadcasted_iota(jnp.int32, (suffix_rows, suffix_rows), 1) <= lax.broadcasted_iota(
        jnp.int32, (suffix_rows, suffix_rows), 0
    )

    lane = lax.broadcasted_iota(jnp.int32, (suffix_rows, HD), 1)

    def scores(h):
        s = lax.dot_general(
            q_ref[:, h * HD : (h + 1) * HD], kbuf[...], NT, preferred_element_type=jnp.float32
        )
        return jnp.concatenate(
            [s[:, :prefix_rows], jnp.where(causal, s[:, prefix_rows:], LOW)], axis=1
        )

    def finish(s, h):
        peak = jnp.max(s, axis=1, keepdims=True)
        weights = jnp.exp2((s - peak) * SCALE).astype(jnp.bfloat16)
        mixed = jnp.dot(weights, vbuf[...], preferred_element_type=jnp.float32)
        o_ref[:, h * HD : (h + 1) * HD] = mixed[:, :HD]
        held = jnp.where(lane == GROUPS + h, mixed[:, HD:], stat_ref[...])
        stat_ref[...] = jnp.where(lane == h, peak, held)

    pipelined(scores, finish)


def attend_text(me, length, queries, prefix, suffix):
    rows = queries.shape[0]
    total, wide = prefix[0].shape[0] + suffix.shape[0], GROUPS * HD
    column = lambda g, *_: (0, g)
    return pl.pallas_call(
        functools.partial(text_kernel, len(prefix)),
        out_shape=[
            jax.ShapeDtypeStruct(queries.shape, jnp.float32),
            jax.ShapeDtypeStruct((rows, KVH * HD), jnp.float32),
            jax.ShapeDtypeStruct((KVH, total, 2 * HD), queries.dtype),
        ],
        grid_spec=pltpu.PrefetchScalarGridSpec(
            num_scalar_prefetch=2,
            grid=(KVH,),
            in_specs=[pl.BlockSpec((rows, wide), column)]
            + [pl.BlockSpec(block.shape, lambda g, *_: (0, 0)) for block in prefix]
            + [
                pl.BlockSpec((suffix.shape[0], HD), column),
                pl.BlockSpec((suffix.shape[0], HD), lambda g, *_: (0, KVH + g)),
            ],
            out_specs=[
                pl.BlockSpec((rows, wide), column),
                pl.BlockSpec((rows, HD), column),
                pl.BlockSpec((1, total, 2 * HD), lambda g, *_: (g, 0, 0)),
            ],
            scratch_shapes=[
                pltpu.VMEM((len(prefix),) + prefix[0].shape, queries.dtype),
                pltpu.VMEM((total, HD), queries.dtype),
                pltpu.VMEM((total, 2 * HD), queries.dtype),
            ],
        ),
        compiler_params=PARAMS,
        cost_estimate=lasting(21),
        name="attend_text",
    )(me, length, queries, *prefix, suffix, suffix)


def tile_at(tiles, n):
    return tiles[n // 2].at[n % 2]


def place_tiles(slots, kept, tiles, place_ref):
    count = jnp.int32(0)
    for n in range(slots):
        found = jnp.max(tile_at(tiles, n)[0:1, :HD].astype(jnp.float32)) < EMPTY
        place_ref[n] = jnp.where(found, count, kept)
        count = count + jnp.where(found, 1, 0)


def fill_image(slots, head, tiles, place_ref, kbuf, vbuf):
    tile_rows = tiles[0].shape[-2]
    for n in range(slots):
        row = pl.ds(pl.multiple_of(place_ref[n] * tile_rows, tile_rows), tile_rows)
        tile = tile_at(tiles, n)
        for i, buf in enumerate((kbuf, vbuf)):
            first = (2 * head + i) * HD
            buf[row, :HD] = tile[:, first : first + HD]


def image_kernel(slots, kept, count, last, q_ref, acc_ref, stat_ref, *rest):
    tiles, rest = rest[:count], rest[count:]
    if last:
        length, last_ref, head_ref, text_ref, o_ref, score_ref, kbuf, vbuf, place_ref = rest[:9]
        kv_ref, sem = rest[9:]
        head_from, heads, prefix_rows = last
        copy = pltpu.make_async_copy(text_ref.at[pl.ds(head_from, heads)], kv_ref, sem)
    else:
        o_ref, kbuf, vbuf, place_ref = rest[-4:]
    tile_rows = tiles[0].shape[-2]
    total, rows = kept * tile_rows, q_ref.shape[0]
    g = pl.program_id(0)

    @pl.when(g == 0)
    def _():
        vbuf[:, :, HD:] = jnp.ones(vbuf.shape[:2] + (HD,), vbuf.dtype)
        place_tiles(slots, kept, tiles, place_ref)
        if last:
            copy.start()

    fill_image(slots, 0, tiles, place_ref, kbuf.at[g], vbuf.at[g])

    def scores(column):
        return lax.dot_general(
            q_ref[:, column], kbuf[g, :total], NT, preferred_element_type=jnp.float32
        )

    def close(summed, totals, column):
        o_ref[:, column] = (summed / totals).astype(o_ref.dtype)

    largest = [jnp.zeros((8, HD), jnp.float32)]

    def finish(s, h):
        column = slice(h * HD, (h + 1) * HD)
        held = stat_ref[:, h : h + 1]
        powers = []
        for k in range(total // HD):
            power = (s[:, k * HD : (k + 1) * HD] - held) * SCALE
            powers.append(jnp.exp2(power).astype(jnp.bfloat16))
        weights = jnp.concatenate(powers, axis=1)
        mixed = jnp.dot(weights, vbuf[g, :total], preferred_element_type=jnp.float32)
        totals = mixed[:, HD:] + stat_ref[:, GROUPS + h : GROUPS + h + 1]
        largest[0] = jnp.maximum(largest[0], jnp.max(totals.reshape(rows // 8, 8, HD), axis=0))
        close(mixed[:, :HD] + acc_ref[:, column], totals, column)

    pipelined(lambda h: scores(slice(h * HD, (h + 1) * HD)), finish)

    @pl.when(jnp.logical_not(jnp.max(largest[0]) < ROOM))
    def _():
        @pl.loop(0, GROUPS)
        def _(h):
            column = pl.ds(pl.multiple_of(h * HD, HD), HD)
            s = scores(column)
            lane = lax.broadcasted_iota(jnp.int32, (rows, HD), 1)
            held = jnp.sum(jnp.where(lane == h, stat_ref[...], 0.0), axis=1, keepdims=True)
            sums = jnp.where(lane == GROUPS + h, stat_ref[...], 0.0)
            sums = jnp.sum(sums, axis=1, keepdims=True)
            peak = jnp.maximum(held, jnp.max(s, axis=1, keepdims=True))
            weights = jnp.exp2((s - peak) * SCALE).astype(jnp.bfloat16)
            mixed = jnp.dot(weights, vbuf[g, :total], preferred_element_type=jnp.float32)
            fade = jnp.exp2((held - peak) * SCALE)
            summed = acc_ref[:, column] * fade + mixed[:, :HD]
            close(summed, sums * fade + mixed[:, HD:], column)

    if last:
        @pl.when(g == heads - 1)
        def _():
            copy.wait()
            score_ref[...] = last_row_gain(
                head_from, heads, prefix_rows, total, length, last_ref, head_ref, kv_ref, kbuf, vbuf
            )


def attend_image(chips, kept, part, tiles, queries, summed, stats, context=None, last=None):
    head_from, heads = part
    tile_rows = tiles[0].shape[-2]
    total, wide, rows = kept * tile_rows, GROUPS * HD, queries.shape[0]
    column = lambda g: (0, head_from + g)
    specs = [pl.BlockSpec((rows, wide), column)] * 2 + [pl.BlockSpec((rows, HD), column)]
    specs += [pl.BlockSpec((2, tile_rows, 2 * HD), lambda g: (0, 0, g)) for tile in tiles]
    operands = [queries, summed, stats, *tiles]
    shapes = [jax.ShapeDtypeStruct(queries.shape, queries.dtype)]
    outs = [pl.BlockSpec((rows, wide), column)]
    scratch = [
        pltpu.VMEM((heads, total + tile_rows, HD), queries.dtype),
        pltpu.VMEM((heads, total + tile_rows, 2 * HD), queries.dtype),
        pltpu.SMEM((2 * chips,), jnp.int32),
    ]
    aliases, static = {}, None
    if last is not None:
        length, prefix_rows, head, text_rows = last
        static = (head_from, heads, prefix_rows)
        end = rows // LAST - 1
        operands += [length, queries, head, text_rows]
        specs += [
            pl.BlockSpec(memory_space=pltpu.SMEM),
            pl.BlockSpec((LAST, queries.shape[1]), lambda g: (end, 0)),
            pl.BlockSpec(head.shape, lambda g: (0, 0)),
            pl.BlockSpec(memory_space=pl.ANY),
        ]
        shapes.append(jax.ShapeDtypeStruct((GROUPS, HD), jnp.float32))
        outs.append(pl.BlockSpec((GROUPS, HD), lambda g: (0, 0)))
        scratch += [
            pltpu.VMEM((heads,) + text_rows.shape[1:], queries.dtype),
            pltpu.SemaphoreType.DMA,
        ]
    if context is not None:
        aliases = {len(operands): 0}
        operands.append(context)
        specs.append(pl.BlockSpec(memory_space=pl.ANY))
    return pl.pallas_call(
        functools.partial(image_kernel, 2 * chips, kept, len(tiles), static),
        out_shape=shapes,
        grid=(heads,),
        in_specs=specs,
        out_specs=outs,
        scratch_shapes=scratch,
        input_output_aliases=aliases,
        compiler_params=PARAMS,
        cost_estimate=lasting(2 * heads),
        name="attend_image",
    )(*operands)


def last_row_gain(
    head_from, heads, prefix_rows, total, length, q_ref, head_ref, kv_ref, kbuf, vbuf
):
    gain = jnp.zeros((GROUPS, HD), jnp.float32)
    column = lax.broadcasted_iota(jnp.int32, (GROUPS, kv_ref.shape[1]), 1)
    live = (column < length[0]) | (column >= prefix_rows)
    for i in range(heads):
        first = (head_from + i) * GROUPS
        q = [q_ref[:, (first + h) * HD : (first + h + 1) * HD] for h in range(GROUPS)]
        q = jnp.concatenate([part.astype(jnp.float32)[-1:] for part in q], axis=0)
        q = q.astype(jnp.bfloat16)
        s = [
            lax.dot_general(q, keys, NT, preferred_element_type=jnp.float32)
            for keys in (kv_ref[i, :, :HD], kbuf[i, :total])
        ]
        s[0] = jnp.where(live, s[0], LOW)
        peak = jnp.maximum(*[jnp.max(part, axis=1, keepdims=True) for part in s])
        weights = [jnp.exp2((part - peak) * SCALE) for part in s]
        mixed = sum(
            jnp.dot(part.astype(jnp.bfloat16), values, preferred_element_type=jnp.float32)
            for part, values in zip(weights, (kv_ref[i, :, HD:], vbuf[i, :total, :HD]))
        )
        totals = sum(jnp.sum(part, axis=1, keepdims=True) for part in weights)
        out = (mixed / totals).astype(jnp.bfloat16).astype(jnp.float32)
        gain = gain + out * head_ref[first : first + GROUPS, :]
    return gain


def last_kernel(slots, kept, count, head_from, heads, prefix_rows, length, q_ref, head_ref, kv_ref, *rest):
    tiles, (before, score_ref, kbuf, vbuf, place_ref) = rest[:count], rest[count:]
    total = kept * tiles[0].shape[-2]
    place_tiles(slots, kept, tiles, place_ref)
    for i in range(heads):
        fill_image(slots, i, tiles, place_ref, kbuf.at[i], vbuf.at[i])
    gain = before[...] + last_row_gain(
        head_from, heads, prefix_rows, total, length, q_ref, head_ref, kv_ref, kbuf, vbuf
    )
    score_ref[...] = jnp.broadcast_to(jnp.sum(gain, axis=0, keepdims=True), score_ref.shape)


def last_scratch(heads, rows, dtype):
    return [pltpu.VMEM((heads, rows, HD), dtype)] * 2


def last_rows(chips, kept, part, tiles, queries, length, prefix_rows, head, text_rows, share, devices):
    head_from, heads = part
    tile_rows, text = tiles[0].shape[-2], text_rows.shape[1]
    whole = lambda x: pl.BlockSpec(x.shape, lambda g, d=x.ndim: (0,) * d)
    end = queries.shape[0] // LAST - 1
    specs = [
        pl.BlockSpec(memory_space=pltpu.SMEM),
        pl.BlockSpec((LAST, queries.shape[1]), lambda g: (end, 0)),
        whole(head),
        pl.BlockSpec(
            (pl.Element(heads), pl.Element(text), pl.Element(2 * HD)), lambda g: (head_from, 0, 0)
        ),
    ]
    shape = (devices, HD)
    return pl.pallas_call(
        functools.partial(
            last_kernel, 2 * chips, kept, len(tiles), head_from, heads, prefix_rows
        ),
        out_shape=jax.ShapeDtypeStruct(shape, jnp.float32),
        grid=(1,),
        in_specs=specs + [whole(tile) for tile in tiles] + [whole(share)],
        out_specs=pl.BlockSpec(shape, lambda g: (0, 0)),
        scratch_shapes=last_scratch(heads, (kept + 1) * tile_rows, queries.dtype)
        + [pltpu.SMEM((2 * chips,), jnp.int32)],
        compiler_params=PARAMS,
        cost_estimate=lasting(heads),
        name="last_rows",
    )(length, queries, head, text_rows, *tiles, share)


def normalize_kernel(prompts, slots, every_ref, out_ref):
    own = lax.axis_index("prompt") * slots + lax.axis_index("slot")
    score = jnp.sum(every_ref[...], axis=1, keepdims=True)
    score = jnp.broadcast_to(score, every_ref.shape).reshape(prompts, slots, HD)
    deviation = score - jnp.sum(score, axis=1, keepdims=True) / slots
    spread = jnp.sum(jnp.sum(deviation * deviation, axis=0), axis=0, keepdims=True)
    advantage = deviation / jnp.sqrt(spread / (prompts * slots) + 1e-06)
    advantage = advantage.reshape(prompts * slots, HD)
    row = lax.broadcasted_iota(jnp.int32, advantage.shape, 0)
    out_ref[...] = jnp.sum(jnp.where(row == own, advantage, 0.0), axis=0, keepdims=True)[:, :1]


def per_device(patch_kv, routes, prefix_kv, prefix_len, queries, suffix_kv, score_head):
    slot_count = lax.axis_size("slot")
    prompt_count = lax.axis_size("prompt")
    chips = slot_count // 2
    kept = slot_count // 2
    me = lax.axis_index("slot").astype(jnp.int32).reshape(1)

    def swap(x, k):
        return lax.ppermute(x, "slot", [(i, i ^ k) for i in range(slot_count)])

    slot = jnp.arange(routes.shape[1], dtype=jnp.int32)
    judges = 2 * (jnp.arange(chips, dtype=jnp.int32) ^ (me // 2)) + me % 2
    held, for_mate = [
        jnp.max(jnp.where(routes == judge[:, None], slot, -1), axis=1)
        for judge in (judges, judges ^ 1)
    ]
    mate_patch, mate_held = swap(patch_kv[0], 1), swap(for_mate, 1)
    near = [prefix_kv[0]] + [swap(prefix_kv[0], 2 * offset) for offset in range(1, chips)]
    buffers = pack(PARTS, chips, held, mate_held, patch_kv[0], mate_patch)
    come = lax.optimization_barrier((near[1:], buffers[0]))[0]
    far = [swap(block, 1) for block in [near[0], *come]]
    first, second = list(buffers[:chips]), list(buffers[chips:])
    for n in range(1, chips):
        first[n] = lax.optimization_barrier((first[n], near[:-1] if n == chips - 1 else near))[0]
    prefix = [block for pair in zip(near, far) for block in pair]
    suffix = suffix_kv[0, 0]
    summed, stats, text_rows = attend_text(me, prefix_len, queries[0, 0], prefix, suffix)

    second[-1] = lax.optimization_barrier((second[-1], stats))[0]
    arrived = [
        [sent[0]] + [swap(sent[offset], 2 * offset) for offset in range(1, chips)]
        for sent in (first, second)
    ]
    head = score_head.reshape(HEADS, HD)
    last = (prefix_len, prefix_kv.shape[1], head, text_rows)
    main = (queries[0, 0], summed, stats)
    context, share = attend_image(chips, kept, PARTS[0], arrived[0], *main, last=last)
    devices = prompt_count * slot_count
    shares = last_rows(chips, kept, PARTS[1], arrived[1], queries[0, 0], *last, share, devices)
    every = lax.all_to_all(shares, ("prompt", "slot"), 0, 0, tiled=True)
    (context,) = attend_image(chips, kept, PARTS[1], arrived[1], *main, context)
    advantage = pl.pallas_call(
        functools.partial(normalize_kernel, prompt_count, slot_count),
        out_shape=jax.ShapeDtypeStruct((1, 1), jnp.float32),
        in_specs=[pl.BlockSpec(memory_space=pltpu.VMEM)],
        out_specs=pl.BlockSpec(memory_space=pltpu.VMEM),
        cost_estimate=lasting(1),
        name="normalize",
    )(every)
    return (context[None, None], advantage)


def solution(mesh):
    placed = (
        P("prompt", "slot", None, None),
        P("prompt", "slot"),
        P("prompt", None, "slot"),
        P("prompt"),
        P("prompt", "slot", None, None),
        P("prompt", "slot", None, None),
        P(),
    )
    return jax.shard_map(
        per_device,
        mesh=mesh,
        in_specs=placed,
        out_specs=(P("prompt", "slot", None, None), P("prompt", "slot")),
        check_vma=False,
    )
```
